128 devices in a mesh: dp: 32 (over z, y, x_lo), section: 2 (over core), tensor: 2 (over x_hi).
Axes of the slice: x: 4 (x_hi: 2, x_lo: 2; x = x_hi * 2 + x_lo), y: 4, z: 4, core: 2. Of those that a mesh axis runs over, the one named last changes fastest.
Arguments:
- llm_grad: bfloat16 [2, 2048, 5120], P(None, 'dp', 'tensor'), may hold values from -6 to 6
- slots: int32 [2, 1536], P(None, 'dp'), may hold values from 0 to 2047, as said below
- frames: int32 [2, 64], P(None, 'dp'), may hold values from 0 to 12, as said below
- saved_in: bfloat16 [2, 2, 6144, 1280], P('section', None, 'dp'), may hold values from -6 to 6
- ln_gain: float32 [2, 1280], P('section'), may hold values from 0.1 to 1.9
- w_in: bfloat16 [2, 1280, 5120], P('section', None, 'tensor'), may hold values from -0.15625 to 0.15625
- w_out: bfloat16 [2, 5120, 1280], P('section', 'tensor'), may hold values from -0.078125 to 0.078125
Outputs:
- input_grads: bfloat16 [2, 2, 6144, 1280], P('section', None, 'dp')
- grad_in: bfloat16 [2, 1280, 5120], P('section', 'dp', 'tensor')
- grad_out: bfloat16 [2, 5120, 1280], P('section', 'tensor', 'dp')
The draws below stay inside these ranges and needn't reach their ends.
Inputs may be any that keep to these rules, and one draw needn't show every extreme that they name: `frames`: within a replica's 2 samples of one micro-batch the frame counts sum to at most 12, and exactly one replica of each micro-batch reaches it; over all replicas of one micro-batch they sum to 132. Slot j of replica r holds one of the 64 positions of replica (r + j) mod 32; all slots of one micro-batch are distinct positions.
All inputs are finite; a program needn't handle non-finite values.
Results may differ from the reference program's by a relative error of at most 0.034.
Values may be sent and summed in bfloat16 or wider, within the bound.
No kernel may reach another device: no remote copies, remote signals or barrier semaphores. Data moves between devices by JAX's collectives and lax.ppermute only.
A program may use at most 128 MiB of HBM per device.

```python
import jax
import jax.numpy as jnp
from jax import lax

D = 1280
FF = 5120
TPF = 4
SAMP = 2
MB = 2
MT_DEV = 16
CAP = 48
TOK = 192
SEQ_DEV = 64
SEQ = 2048
SECTIONS = 2
N_DP = 32
N_TENSOR = 2


def draw_frames(key, part):
    key = jax.random.fold_in(key, 11)
    mean_frames = MT_DEV // TPF
    blocks = []
    for micro in range(MB):
        sub = jax.random.fold_in(key, micro)
        key_order, key_split = jax.random.split(sub)
        order = jax.random.permutation(key_order, N_DP)
        place = jnp.argsort(order).astype(jnp.int32)
        extra = jnp.where((place >= 4) & ((place - 4) % 2 == 0) & (place + 1 < N_DP), 1, 0)
        extra = extra - jnp.where((place >= 5) & ((place - 5) % 2 == 0), 1, 0)
        totals = jnp.where(place == 0, 3 * mean_frames, jnp.where(place == 1, mean_frames - 2, jnp.where(place <= 3, mean_frames - 1, mean_frames + extra)))
        first = jax.random.randint(key_split, (N_DP,), 0, totals + 1)
        first = jnp.where(place == 0, totals, first)
        blocks.append(jnp.stack([first, totals - first], axis=1).reshape(N_DP * SAMP))
    return jnp.stack(blocks).astype(jnp.int32)


def roll_front(values, shift_by):
    return jnp.roll(values, -shift_by)


def draw_slots(key, part):
    key = jax.random.fold_in(key, 12)
    blocks = []
    owners = jnp.arange(N_DP, dtype=jnp.int32)
    target = jnp.where(owners == N_DP - 1, SEQ_DEV - 1, 0).astype(jnp.int32)
    for micro in range(MB):
        sub = jax.random.fold_in(key, micro)
        keys = jax.random.split(sub, N_DP)
        perms = jax.vmap(lambda one_key: jax.random.permutation(one_key, SEQ_DEV))(keys).astype(jnp.int32)
        where_target = jnp.argmax((perms == target[:, None]).astype(jnp.int32), axis=1).astype(jnp.int32)
        rolled = jax.vmap(roll_front)(perms, where_target)
        replica = jnp.arange(N_DP, dtype=jnp.int32)[:, None]
        within = jnp.arange(CAP, dtype=jnp.int32)[None, :]
        holder = (replica + within) % N_DP
        slot = holder * SEQ_DEV + rolled[holder, within]
        blocks.append(slot.reshape(N_DP * CAP))
    return jnp.stack(blocks).astype(jnp.int32)


def level_of(stream_key, extent, cuts, smallest, top_value):
    loudness, own = 1.0, jax.random.fold_in(stream_key, 6)
    for dim, shards_of in cuts:
        draws = jnp.exp(jax.random.uniform(jax.random.fold_in(own, dim), (shards_of,), jnp.float32, smallest / len(cuts), top_value / len(cuts)))
        loudness = loudness * jnp.repeat(draws, extent[dim] // shards_of).reshape([-1 if axis == dim else 1 for axis in range(len(extent))])
    return loudness


def gaussian(key, extent, deviation, limit, shards=(), held_as=jnp.bfloat16):
    factor_of = level_of(key, extent, shards, -0.22, 0.18) if shards else 1.0
    entries = jax.random.normal(key, extent, jnp.float32) * deviation * factor_of
    return jnp.minimum(jnp.maximum(entries, -limit), limit).astype(held_as)


def setup_inputs(seed: int = 0) -> dict:
    streams_of = jax.random.split(jax.random.key(seed), 8)
    return {
        "llm_grad": gaussian(streams_of[0], (MB, SEQ, 4 * D), 1.0, 6.0, ((1, 32), (2, 2))),
        "slots": draw_slots(jax.random.fold_in(streams_of[7], 71), 0),
        "frames": draw_frames(jax.random.fold_in(streams_of[7], 71), 0),
        "saved_in": gaussian(streams_of[3], (SECTIONS, MB, N_DP * TOK, D), 1.0, 6.0, ((0, 2), (2, 32))),
        "ln_gain": jnp.clip(1.0 + 0.18 * jax.random.normal(streams_of[4], (SECTIONS, D), jnp.float32), 0.1, 1.9),
        "w_in": gaussian(streams_of[5], (SECTIONS, D, FF), D ** -0.5, 0.15625, ((0, 2), (2, 2))),
        "w_out": gaussian(streams_of[6], (SECTIONS, FF, D), FF ** -0.5, 0.078125, ((0, 2), (1, 2))),
    }


def gelu_slope(values):
    inner = 0.7978845608 * (values + 0.044715 * values * values * values)
    tangent = jnp.tanh(inner)
    return 0.5 * (1.0 + tangent) + 0.5 * values * (1.0 - tangent * tangent) * 0.7978845608 * (1.0 + 3.0 * 0.044715 * values * values)

def block_back(inputs_now, upstream_gradient, norm_gain_vector, weight_in, weight_out):
    widen = inputs_now.astype(jnp.float32)
    centered_input = widen - lax.optimization_barrier(jnp.mean(widen, axis=-1, keepdims=True))
    inverse_deviation = lax.rsqrt(lax.optimization_barrier(jnp.mean(centered_input * centered_input, axis=-1, keepdims=True)) + 1e-05)
    standardized_input = centered_input * inverse_deviation
    normalized_rows = (standardized_input * norm_gain_vector).astype(jnp.bfloat16)
    pre_act = jnp.dot(normalized_rows, weight_in, preferred_element_type=jnp.float32)
    activ = jax.nn.gelu(pre_act, approximate=True).astype(jnp.bfloat16)
    back_act = jnp.dot(upstream_gradient, weight_out.T, preferred_element_type=jnp.float32)
    d_pre = (back_act * gelu_slope(pre_act)).astype(jnp.bfloat16)
    rows_all = d_pre.shape[0]
    split_pre = d_pre.reshape(rows_all, N_TENSOR, FF // N_TENSOR).astype(jnp.float32)
    split_win = weight_in.reshape(D, N_TENSOR, FF // N_TENSOR).astype(jnp.float32)
    partials = jnp.einsum('rkf,dkf->krd', split_pre, split_win)
    d_norm = lax.optimization_barrier(jnp.sum(partials.astype(jnp.bfloat16).astype(jnp.float32), axis=0))
    scaled_rows = d_norm * norm_gain_vector
    input_gradient = upstream_gradient.astype(jnp.float32) + inverse_deviation * (scaled_rows - lax.optimization_barrier(jnp.mean(scaled_rows, axis=-1, keepdims=True)) - standardized_input * lax.optimization_barrier(jnp.mean(scaled_rows * standardized_input, axis=-1, keepdims=True)))
    return (input_gradient.astype(jnp.bfloat16), normalized_rows, d_pre, activ)

def replica_sum(left, right):
    left_r = jnp.moveaxis(left.reshape(MB, N_DP, TOK, left.shape[-1]), 1, 0)
    right_r = jnp.moveaxis(right.reshape(MB, N_DP, TOK, right.shape[-1]), 1, 0)

    def add_one(total, pair):
        term = jnp.einsum('mtd,mtf->df', pair[0].astype(jnp.float32), pair[1].astype(jnp.float32))
        return (total + term.astype(jnp.bfloat16).astype(jnp.float32), None)
    start = jnp.zeros((left.shape[-1], right.shape[-1]), jnp.float32)
    total, _ = lax.scan(add_one, start, (left_r, right_r))
    return total.astype(jnp.bfloat16)

def reference(llm_grad, slots, frames, saved_in, ln_gain, w_in, w_out):
    merged_counts = TPF * lax.optimization_barrier(jnp.sum(frames.reshape(MB, N_DP, SAMP), axis=-1))
    rows = jax.vmap(lambda lookup_table, where_at: lookup_table[where_at])(llm_grad, slots)
    live_mask = (jnp.arange(CAP)[None, None, :] < merged_counts[:, :, None]).reshape(MB, N_DP * CAP)
    pooled_tokens = jnp.where(live_mask[:, :, None], rows, jnp.zeros_like(rows)).astype(jnp.bfloat16)
    upstream_gradient = pooled_tokens.reshape(MB, N_DP * TOK, D)
    grads_by_block = [None] * SECTIONS
    grads_win = [None] * SECTIONS
    grads_wout = [None] * SECTIONS
    for block_num in reversed(range(SECTIONS)):
        d_list, n_list, p_list, a_list = ([], [], [], [])
        for micro in range(MB):
            input_gradient, normalized_rows, d_pre, activ = block_back(saved_in[block_num, micro], upstream_gradient[micro], ln_gain[block_num], w_in[block_num], w_out[block_num])
            d_list.append(input_gradient)
            n_list.append(normalized_rows)
            p_list.append(d_pre)
            a_list.append(activ)
        block_grads = jnp.stack(d_list)
        grads_win[block_num] = replica_sum(jnp.stack(n_list), jnp.stack(p_list))
        grads_wout[block_num] = replica_sum(jnp.stack(a_list), upstream_gradient)
        grads_by_block[block_num] = block_grads
        upstream_gradient = block_grads
    return (jnp.stack(grads_by_block), jnp.stack(grads_win), jnp.stack(grads_wout))
```

```python
import jax
import jax.numpy as jnp
from jax import lax
from jax.sharding import PartitionSpec as P

TPF = 4
BITS = 5


def gelu_slope(values):
    inner = 0.7978845608 * (values + 0.044715 * values * values * values)
    tangent = jnp.tanh(inner)
    return 0.5 * (1.0 + tangent) + 0.5 * values * (1.0 - tangent * tangent) * 0.7978845608 * (
        1.0 + 3.0 * 0.044715 * values * values
    )


def split_index(r):
    return r // 8, (r // 2) % 4, r % 2


def to_code(r):
    z, y, x = split_index(r)
    return ((z ^ (z >> 1)) << 3) | ((y ^ (y >> 1)) << 1) | x


def from_code(q):
    gz, gy, x = q >> 3, (q >> 1) & 3, q & 1
    return ((gz ^ (gz >> 1)) << 3) | ((gy ^ (gy >> 1)) << 1) | x


def neighbour_pairs(bit):
    return [(r, from_code(to_code(r) ^ (1 << (BITS - 1 - bit)))) for r in range(1 << BITS)]


def dot(a, b, ca, cb):
    return lax.dot_general(a, b, (((ca,), (cb,)), ((), ())), preferred_element_type=jnp.float32)


def fetch_tokens(llm_grad, slots, frames, sec, ten, rep, peers):
    seq_dev, width = llm_grad.shape[1:]
    cap = slots.shape[1]
    per = -(-cap // peers)
    counts = TPF * jnp.sum(frames, axis=1)
    count = lax.dynamic_index_in_dim(counts, sec, 0, keepdims=False)
    wanted = lax.dynamic_index_in_dim(slots, sec, 0, keepdims=False)
    wanted = jnp.concatenate([wanted, jnp.zeros((per * peers - cap,), jnp.int32)])
    j = jnp.arange(per * peers)
    position = jnp.where(j < count, wanted - seq_dev * ((rep + j) % peers) + 1, 0)
    position = position.reshape(per, 1, peers)
    holder = jnp.arange(peers)
    turned = (jnp.arange(peers)[None, :] == ((holder - rep) % peers)[:, None]).astype(jnp.int32)
    requests = jnp.sum(position * turned[None], axis=2).T
    asked = lax.all_to_all(requests, "dp", 0, 0, tiled=True).reshape(-1)
    pick = (asked[:, None] == jnp.arange(1, seq_dev + 1)[None, :]).astype(jnp.bfloat16)
    held = lax.dynamic_index_in_dim(llm_grad, sec, 0, keepdims=False)
    rows = dot(pick, held, 1, 0).astype(jnp.bfloat16)
    got = lax.all_to_all(rows, "dp", 0, 0, tiled=True)
    both = ("section", "tensor")
    first_own = lax.ppermute(got, both, [(0, 2), (1, 3)])
    first_other = lax.ppermute(got, both, [(0, 3), (1, 2)])
    second_other = lax.ppermute(got, both, [(2, 3), (3, 2)])
    half = width // 2
    row = jnp.arange(cap * 4)
    tok, part = row // 4, row % 4
    source = (
        ((part // 2 != ten).astype(jnp.int32) * 2 + part % 2) * (per * peers)
        + ((rep + tok) % peers) * per
        + tok // peers
    )
    spread = (source[:, None] == jnp.arange(4 * per * peers)[None, :]).astype(jnp.bfloat16)
    out = []
    for own, other in ((first_own, first_other), (got, second_other)):
        stacked = jnp.concatenate([own[:, :half], own[:, half:], other[:, :half], other[:, half:]])
        out.append(dot(spread, stacked, 1, 0).astype(jnp.bfloat16))
    return jnp.concatenate(out)


def reduce_weight_grads(left, right):
    width, columns = left.shape[1], right.shape[2]
    chunk = width >> BITS
    span = columns // BITS
    parts = []
    for i in range(BITS):
        ordered = (
            left.reshape(2, 1 << i, 1 << (BITS - i), chunk, -1).swapaxes(1, 2).reshape(left.shape)
        )
        right_i = right[:, :, i * span : (i + 1) * span]

        def group(lo, hi, received):
            total = lax.dot_general(
                ordered[:, lo:hi],
                right_i,
                (((2,), (1,)), ((0,), (0,))),
                preferred_element_type=jnp.float32,
            )
            for piece in received:
                total = total + piece[:, lo:hi].astype(jnp.float32)
            return total.astype(jnp.bfloat16)

        received = []
        for t in range(BITS):
            send = group(width >> (t + 1), width >> t, received)
            received.append(lax.ppermute(send, "dp", neighbour_pairs((i + t) % BITS)))
        parts.append(group(0, chunk, received))
    return jnp.concatenate(parts, axis=2)


def per_device(llm_grad, slots, frames, saved_in, ln_gain, w_in, w_out):
    peers = lax.axis_size("dp")
    sec = lax.axis_index("section")
    ten = lax.axis_index("tensor")
    rep = lax.axis_index("dp")
    micro_count, tok_rows, width = saved_in.shape[1:]
    rows = micro_count * tok_rows
    gain = ln_gain[0]
    weight_in = w_in[0]
    weight_out = w_out[0]

    upstream = fetch_tokens(llm_grad, slots, frames, sec, ten, rep, peers)

    widen = saved_in[0].reshape(rows, width).astype(jnp.float32)
    centered = widen - jnp.mean(widen, axis=-1, keepdims=True)
    rstd = lax.rsqrt(jnp.mean(centered * centered, axis=-1, keepdims=True) + 1e-05)
    xhat = centered * rstd
    normed = (xhat * gain).astype(jnp.bfloat16)
    pre_act = dot(normed, weight_in, 1, 0)
    activ = jax.nn.gelu(pre_act, approximate=True).astype(jnp.bfloat16)
    slope = gelu_slope(pre_act)

    order = from_code(to_code(rep) ^ jnp.arange(peers))
    chunk = width // peers
    order = (order[:, None] * chunk + jnp.arange(chunk)[None, :]).reshape(-1)
    turn = (order[:, None] == jnp.arange(width)[None, :]).astype(jnp.bfloat16)
    normed_t = dot(turn, normed, 1, 1).astype(jnp.bfloat16)

    def back(incoming):
        d_pre = (dot(incoming, weight_out, 1, 1) * slope).astype(jnp.bfloat16)
        return d_pre, dot(d_pre, weight_in, 1, 1).astype(jnp.bfloat16)

    def input_gradient(incoming, mine, other):
        d_norm = mine.astype(jnp.float32) + other.astype(jnp.float32)
        scaled = d_norm * gain
        return (
            incoming.astype(jnp.float32)
            + rstd
            * (
                scaled
                - jnp.mean(scaled, axis=-1, keepdims=True)
                - xhat * jnp.mean(scaled * xhat, axis=-1, keepdims=True)
            )
        ).astype(jnp.bfloat16)

    both = ("section", "tensor")
    _, partial = back(upstream)
    other = lax.ppermute(partial, both, [(2, 3), (3, 2)])
    grad_last = input_gradient(upstream, partial, other)
    passed = lax.ppermute(grad_last, "section", [(1, 0)])
    incoming = jnp.where(sec == 1, upstream, passed)
    d_pre, partial = back(incoming)
    other = lax.ppermute(partial, both, [(0, 1), (1, 0)])
    grad_here = input_gradient(incoming, partial, other)
    results = jnp.where(sec == 1, grad_last, grad_here)

    incoming_t = dot(turn, incoming, 1, 1).astype(jnp.bfloat16)
    reduced = reduce_weight_grads(
        jnp.stack([normed_t, incoming_t]), jnp.stack([d_pre, activ])
    )
    return (
        results.reshape(1, micro_count, tok_rows, width),
        reduced[0][None],
        reduced[1].T[None],
    )


def solution(mesh):
    return jax.shard_map(
        per_device,
        mesh=mesh,
        in_specs=(
            P(None, "dp", "tensor"),
            P(None, "dp"),
            P(None, "dp"),
            P("section", None, "dp", None),
            P("section", None),
            P("section", None, "tensor"),
            P("section", "tensor", None),
        ),
        out_specs=(
            P("section", None, "dp", None),
            P("section", "dp", "tensor"),
            P("section", "tensor", "dp"),
        ),
        check_vma=False,
    )
```

```python
import jax
import jax.numpy as jnp
from jax import lax
from jax.experimental import pallas as pl
from jax.experimental.pallas import tpu as pltpu
from jax.sharding import PartitionSpec as P

TPF = 4
BITS = 5
ORDERS = ((0, 1, 2, 3, 4), (1, 2, 0, 3, 4), (2, 3, 4, 0, 1), (3, 4, 2, 0, 1), (4, 0, 1, 2, 3))
SHARED = (
    ((0,), (1,), (2,), (3,), (4,)),
    ((0,), (1,), (2,), (3,), (4,)),
    ((0, 3), (1,), (2,), (4,)),
    ((0, 1), (2, 3), (4,)),
    ((0, 1), (2, 3), (4,)),
)
LAYOUTS = (
    ((32,), (0,)),
    ((2, 4, 4), (1, 0, 2)),
    ((4, 8), (1, 0)),
    ((4, 2, 4), (2, 1, 0)),
    ((16, 2), (1, 0)),
)


def gelu_and_slope(a):
    square = a * a
    tangent = jnp.tanh(0.7978845608 * a * (1.0 + 0.044715 * square))
    half = 0.5 * (1.0 + tangent)
    slope = half + (0.5 * 0.7978845608) * a * (1.0 - tangent * tangent) * (
        1.0 + (3.0 * 0.044715) * square
    )
    return (a * half).astype(jnp.bfloat16), slope.astype(jnp.bfloat16)


def split_index(r):
    return r // 8, (r // 2) % 4, r % 2


def to_code(r):
    z, y, x = split_index(r)
    return ((z ^ (z >> 1)) << 3) | ((y ^ (y >> 1)) << 1) | x


def from_code(q):
    gz, gy, x = q >> 3, (q >> 1) & 3, q & 1
    return ((gz ^ (gz >> 1)) << 3) | ((gy ^ (gy >> 1)) << 1) | x


def neighbour_pairs(bit):
    return [(r, from_code(to_code(r) ^ (1 << (BITS - 1 - bit)))) for r in range(1 << BITS)]


def dot(a, b, ca, cb):
    return lax.dot_general(a, b, (((ca,), (cb,)), ((), ())), preferred_element_type=jnp.float32)


def finish_kernel(g_ref, mine_ref, other_ref, x_ref, gain_ref, out_ref):
    x = x_ref[...].astype(jnp.float32)
    centered = x - jnp.mean(x, axis=-1, keepdims=True)
    rstd = lax.rsqrt(jnp.mean(centered * centered, axis=-1, keepdims=True) + 1e-05)
    xhat = centered * rstd
    scaled = (mine_ref[...].astype(jnp.float32) + other_ref[...].astype(jnp.float32)) * gain_ref[...]
    out_ref[...] = (
        g_ref[...].astype(jnp.float32)
        + rstd
        * (
            scaled
            - jnp.mean(scaled, axis=-1, keepdims=True)
            - xhat * jnp.mean(scaled * xhat, axis=-1, keepdims=True)
        )
    ).astype(jnp.bfloat16)


def finish(incoming, mine, other, x, gain, tile):
    rows, width = incoming.shape
    wide = pl.BlockSpec((tile, width), lambda i: (i, 0))
    return pl.pallas_call(
        finish_kernel,
        grid=(rows // tile,),
        in_specs=[wide, wide, wide, wide, pl.BlockSpec((1, width), lambda i: (0, 0))],
        out_specs=wide,
        out_shape=jax.ShapeDtypeStruct((rows, width), jnp.bfloat16),
        compiler_params=pltpu.CompilerParams(vmem_limit_bytes=8 * 1024 * 1024),
        cost_estimate=pl.CostEstimate(
            flops=20 * rows * width, bytes_accessed=10 * rows * width, transcendentals=0
        ),
    )(incoming, mine, other, x, gain)


def ask_tokens(seq_dev, slots, frames, sec, rep, peers):
    cap = slots.shape[1]
    per = -(-cap // peers)
    counts = TPF * jnp.sum(frames, axis=1)
    count = lax.dynamic_index_in_dim(counts, sec, 0, keepdims=False)
    wanted = lax.dynamic_index_in_dim(slots, sec, 0, keepdims=False)
    wanted = jnp.concatenate([wanted, jnp.zeros((per * peers - cap,), jnp.int32)])
    j = jnp.arange(per * peers)
    position = jnp.where(j < count, wanted - seq_dev * ((rep + j) % peers) + 1, 0)
    position = position.reshape(per, 1, peers)
    holder = jnp.arange(peers)
    turned = (jnp.arange(peers)[None, :] == ((holder - rep) % peers)[:, None]).astype(jnp.int32)
    requests = jnp.sum(position * turned[None], axis=2).T
    return lax.all_to_all(requests, "dp", 0, 0, tiled=True).reshape(-1)


def fetch_tokens(llm_grad, asked, cap, sec, ten, rep, peers):
    seq_dev, width = llm_grad.shape[1:]
    per = -(-cap // peers)
    pick = (asked[:, None] == jnp.arange(1, seq_dev + 1)[None, :]).astype(jnp.bfloat16)
    held = lax.dynamic_index_in_dim(llm_grad, sec, 0, keepdims=False)
    rows = dot(pick, held, 1, 0).astype(jnp.bfloat16)
    got = lax.all_to_all(rows, "dp", 0, 0, tiled=True)
    both = ("section", "tensor")
    first_own = lax.ppermute(got, both, [(0, 2), (1, 3)])
    first_other = lax.ppermute(got, both, [(0, 3), (1, 2)])
    second_other = lax.ppermute(got, both, [(2, 3), (3, 2)])
    half = width // 2
    row = jnp.arange(cap * 4)
    tok, part = row // 4, row % 4
    source = (
        ((part // 2 != ten).astype(jnp.int32) * 2 + part % 2) * (per * peers)
        + ((rep + tok) % peers) * per
        + tok // peers
    )
    spread = (source[:, None] == jnp.arange(4 * per * peers)[None, :]).astype(jnp.bfloat16)
    out = []
    for own, other in ((first_own, first_other), (got, second_other)):
        stacked = jnp.concatenate([own[:, :half], own[:, half:], other[:, :half], other[:, half:]])
        out.append(dot(spread, stacked, 1, 0).astype(jnp.bfloat16))
    return jnp.concatenate(out)


def reordered(left, stream):
    width = left.shape[1]
    sizes, axes = LAYOUTS[stream]
    split = left.reshape((2,) + sizes + (width >> BITS, -1))
    axes = (0,) + tuple(1 + a for a in axes) + (len(axes) + 1, len(axes) + 2)
    return split.transpose(axes).reshape(left.shape)


def after(value, *others):
    return lax.optimization_barrier((value, others))[0]


def reduce_weight_grads(left, right, between):
    width = left.shape[1]
    span = right.shape[2] // BITS
    lefts = [reordered(left, i) for i in range(BITS)]
    received = [[] for _ in range(BITS)]

    def group(i, lo, hi):
        total = lax.dot_general(
            lefts[i][:, lo:hi],
            right[:, :, i * span : (i + 1) * span],
            (((2,), (1,)), ((0,), (0,))),
            preferred_element_type=jnp.float32,
        )
        for piece in received[i]:
            total = total + piece[:, lo:hi].astype(jnp.float32)
        return total.astype(jnp.bfloat16)

    last = None
    for t in range(BITS):
        for streams in SHARED[t]:
            if t:
                for i in streams:
                    received[i][-1] = after(received[i][-1], last)
            sends = [group(i, width >> (t + 1), width >> t) for i in streams]
            last = sends[0] if len(sends) == 1 else jnp.concatenate(sends, axis=2)
            piece = lax.ppermute(last, "dp", neighbour_pairs(ORDERS[streams[0]][t]))
            for k, i in enumerate(streams):
                received[i].append(piece[:, :, k * span : (k + 1) * span])
        if t == 0:
            middle = between(last)
    result = jnp.concatenate([group(i, 0, width >> BITS) for i in range(BITS)], axis=2)
    return result, after(middle, last)


def per_device(llm_grad, slots, frames, saved_in, ln_gain, w_in, w_out):
    peers = lax.axis_size("dp")
    sec = lax.axis_index("section")
    ten = lax.axis_index("tensor")
    rep = lax.axis_index("dp")
    micro_count, tok_rows, width = saved_in.shape[1:]
    rows = micro_count * tok_rows
    gain = ln_gain
    weight_in = w_in[0]
    weight_out = w_out[0]

    widen = saved_in[0].reshape(rows, width).astype(jnp.float32)
    centered = widen - jnp.mean(widen, axis=-1, keepdims=True)
    rstd = lax.rsqrt(jnp.mean(centered * centered, axis=-1, keepdims=True) + 1e-05)
    xhat = centered * rstd
    normed = (xhat * gain).astype(jnp.bfloat16)

    asked = ask_tokens(llm_grad.shape[1], slots, frames, sec, rep, peers)
    normed, asked = lax.optimization_barrier((normed, asked))
    upstream = lax.optimization_barrier(
        fetch_tokens(llm_grad, asked, slots.shape[1], sec, ten, rep, peers)
    )
    activ, slope = lax.optimization_barrier(gelu_and_slope(dot(normed, weight_in, 1, 0)))

    order = from_code(to_code(rep) ^ jnp.arange(peers))
    chunk = width // peers
    order = (order[:, None] * chunk + jnp.arange(chunk)[None, :]).reshape(-1)
    turn = (order[:, None] == jnp.arange(width)[None, :]).astype(jnp.bfloat16)

    x = saved_in[0].reshape(rows, width)

    def pre_gradient(incoming):
        return lax.optimization_barrier(
            (dot(incoming, weight_out, 1, 1) * slope).astype(jnp.bfloat16)
        )

    both = ("section", "tensor")
    first_own = lax.ppermute(got, both, [(0, 2), (1, 3)])
    first_other = lax.ppermute(got, both, [(0, 3), (1, 2)])
    second_other = lax.ppermute(got, both, [(2, 3), (3, 2)])
    half = width // 2
    row = jnp.arange(cap * 4)
    tok, part = row // 4, row % 4
    source = (
        ((part // 2 != ten).astype(jnp.int32) * 2 + part % 2) * (per * peers)
        + ((rep + tok) % peers) * per
        + tok // peers
    )
    spread = (source[:, None] == jnp.arange(4 * per * peers)[None, :]).astype(jnp.bfloat16)
    out = []
    for own, other in ((first_own, first_other), (got, second_other)):
        stacked = jnp.concatenate([own[:, :half], own[:, half:], other[:, :half], other[:, half:]])
        out.append(dot(spread, stacked, 1, 0).astype(jnp.bfloat16))
    return jnp.concatenate(out)


def reordered(left, stream):
    width = left.shape[1]
    sizes, axes = LAYOUTS[stream]
    split = left.reshape((2,) + sizes + (width >> BITS, -1))
    axes = (0,) + tuple(1 + a for a in axes) + (len(axes) + 1, len(axes) + 2)
    return split.transpose(axes).reshape(left.shape)


def after(value, *others):
    return lax.optimization_barrier((value, others))[0]


def reduce_weight_grads(left, right, between):
    width = left.shape[1]
    span = right.shape[2] // BITS
    lefts = [reordered(left, i) for i in range(BITS)]
    received = [[] for _ in range(BITS)]

    def group(i, lo, hi):
        total = lax.dot_general(
            lefts[i][:, lo:hi],
            right[:, :, i * span : (i + 1) * span],
            (((2,), (1,)), ((0,), (0,))),
            preferred_element_type=jnp.float32,
        )
        for piece in received[i]:
            total = total + piece[:, lo:hi].astype(jnp.float32)
        return total.astype(jnp.bfloat16)

    last = None
    for t in range(BITS):
        for streams in SHARED[t]:
            if t:
                for i in streams:
                    received[i][-1] = after(received[i][-1], last)
            sends = [group(i, width >> (t + 1), width >> t) for i in streams]
            last = sends[0] if len(sends) == 1 else jnp.concatenate(sends, axis=2)
            piece = lax.ppermute(last, "dp", neighbour_pairs(ORDERS[streams[0]][t]))
            for k, i in enumerate(streams):
                received[i].append(piece[:, :, k * span : (k + 1) * span])
        if t == 0:
            middle = between(last)
    result = jnp.concatenate([group(i, 0, width >> BITS) for i in range(BITS)], axis=2)
    return result, after(middle, last)


def per_device(llm_grad, slots, frames, saved_in, ln_gain, w_in, w_out):
    peers = lax.axis_size("dp")
    sec = lax.axis_index("section")
    ten = lax.axis_index("tensor")
    rep = lax.axis_index("dp")
    micro_count, tok_rows, width = saved_in.shape[1:]
    rows = micro_count * tok_rows
    gain = ln_gain
    weight_in = w_in[0]
    weight_out = w_out[0]

    widen = saved_in[0].reshape(rows, width).astype(jnp.float32)
    centered = widen - jnp.mean(widen, axis=-1, keepdims=True)
    rstd = lax.rsqrt(jnp.mean(centered * centered, axis=-1, keepdims=True) + 1e-05)
    xhat = centered * rstd
    normed = (xhat * gain).astype(jnp.bfloat16)

    asked = ask_tokens(llm_grad.shape[1], slots, frames, sec, rep, peers)
    normed, asked = lax.optimization_barrier((normed, asked))
    upstream = lax.optimization_barrier(
        fetch_tokens(llm_grad, asked, slots.shape[1], sec, ten, rep, peers)
    )
    activ, slope = lax.optimization_barrier(gelu_and_slope(dot(normed, weight_in, 1, 0)))

    order = from_code(to_code(rep) ^ jnp.arange(peers))
    chunk = width // peers
    order = (order[:, None] * chunk + jnp.arange(chunk)[None, :]).reshape(-1)
    turn = (order[:, None] == jnp.arange(width)[None, :]).astype(jnp.bfloat16)

    x = saved_in[0].reshape(rows, width)

    def pre_gradient(incoming):
        return lax.optimization_barrier(
            (dot(incoming, weight_out, 1, 1) * slope).astype(jnp.bfloat16)
        )

    def operands(incoming, d_pre):
        left = jnp.stack([normed_t, dot(turn, incoming, 1, 1).astype(jnp.bfloat16)])
        return [reordered(left, i) for i in range(BITS)], jnp.stack([d_pre, activ])

    both = ("section", "tensor")
    d_pre = pre_gradient(upstream)
    partial = dot(d_pre, weight_in, 1, 1).astype(jnp.bfloat16)
    other = lax.ppermute(partial, both, [(2, 1), (3, 0)])
    terms, rest = [], ln_gain
    for _ in range(3):
        term = lax.reduce_precision(rest, exponent_bits=8, mantissa_bits=7)
        terms.append(term.astype(jnp.bfloat16))
        rest = rest - term
    packed = jnp.concatenate(
        [partial, upstream, x] + [jnp.broadcast_to(term, (16, width)) for term in terms]
    )
    packed = lax.ppermute(packed, "section", [(1, 0)])
    mine, passed, later_x = (packed[k * rows : (k + 1) * rows] for k in range(3))
    later_gain = sum(
        packed[3 * rows + 16 * k : 3 * rows + 16 * k + 1].astype(jnp.float32) for k in range(3)
    )
    normed_t = dot(turn, after(normed, partial), 1, 1).astype(jnp.bfloat16)
    grad_last = finish(passed, mine, other, later_x, later_gain, tok_rows // 2)

    incoming = jnp.where(sec == 1, upstream, grad_last)
    d_pre = pre_gradient(incoming)
    incoming_t = dot(turn, incoming, 1, 1).astype(jnp.bfloat16)

    def partial_here(last):
        return dot(after(d_pre, last), weight_in, 1, 1).astype(jnp.bfloat16)

    def exchange(last):
        partial = partial_here(last)
        return (
            partial,
            lax.ppermute(partial, both, [(0, 1), (1, 0)]),
            lax.ppermute(after(grad_last, last), "section", [(0, 1)]),
        )

    reduced, (partial, other, returned) = reduce_weight_grads(
        jnp.stack([normed_t, incoming_t]), jnp.stack([d_pre, activ]), exchange
    )
    grad_here = finish(incoming, partial, other, x, ln_gain, tok_rows // 2)
    results = jnp.where(sec == 1, returned, grad_here)
    return (
        results.reshape(1, micro_count, tok_rows, width),
        reduced[0][None],
        reduced[1].T[None],
    )


def solution(mesh):
    return jax.shard_map(
        per_device,
        mesh=mesh,
        in_specs=(
            P(None, "dp", "tensor"),
            P(None, "dp"),
            P(None, "dp"),
            P("section", None, "dp", None),
            P("section", None),
            P("section", None, "tensor"),
            P("section", "tensor", None),
        ),
        out_specs=(
            P("section", None, "dp", None),
            P("section", "dp", "tensor"),
            P("section", "tensor", "dp"),
        ),
        check_vma=False,
    )
```

```python
import jax
import jax.numpy as jnp
from jax import lax
from jax.experimental import pallas as pl
from jax.experimental.pallas import tpu as pltpu
from jax.sharding import PartitionSpec as P

TPF = 4
BITS = 5
ORDERS = ((0, 1, 2, 3, 4), (1, 2, 0, 3, 4), (2, 3, 4, 0, 1), (3, 4, 2, 0, 1), (4, 0, 1, 2, 3))
SHARED = (
    ((0,), (1,), (2,), (3,), (4,)),
    ((0,), (1,), (2,), (3,), (4,)),
    ((0, 3), (1,), (2,), (4,)),
    ((0, 1), (2, 3), (4,)),
    ((0, 1), (2, 3), (4,)),
)
LAYOUTS = (
    ((32,), (0,)),
    ((2, 4, 4), (1, 0, 2)),
    ((4, 8), (1, 0)),
    ((4, 2, 4), (2, 1, 0)),
    ((16, 2), (1, 0)),
)


def gelu_and_slope(a):
    square = a * a
    tangent = jnp.tanh(0.7978845608 * a * (1.0 + 0.044715 * square))
    half = 0.5 * (1.0 + tangent)
    slope = half + (0.5 * 0.7978845608) * a * (1.0 - tangent * tangent) * (
        1.0 + (3.0 * 0.044715) * square
    )
    return (a * half).astype(jnp.bfloat16), slope.astype(jnp.bfloat16)


def split_index(r):
    return r // 8, (r // 2) % 4, r % 2


def to_code(r):
    z, y, x = split_index(r)
    return ((z ^ (z >> 1)) << 3) | ((y ^ (y >> 1)) << 1) | x


def from_code(q):
    gz, gy, x = q >> 3, (q >> 1) & 3, q & 1
    return ((gz ^ (gz >> 1)) << 3) | ((gy ^ (gy >> 1)) << 1) | x


def neighbour_pairs(bit):
    return [(r, from_code(to_code(r) ^ (1 << (BITS - 1 - bit)))) for r in range(1 << BITS)]


def dot(a, b, ca, cb):
    return lax.dot_general(a, b, (((ca,), (cb,)), ((), ())), preferred_element_type=jnp.float32)


def finish_kernel(g_ref, mine_ref, other_ref, x_ref, gain_ref, out_ref):
    x = x_ref[...].astype(jnp.float32)
    centered = x - jnp.mean(x, axis=-1, keepdims=True)
    rstd = lax.rsqrt(jnp.mean(centered * centered, axis=-1, keepdims=True) + 1e-05)
    xhat = centered * rstd
    scaled = (mine_ref[...].astype(jnp.float32) + other_ref[...].astype(jnp.float32)) * gain_ref[...]
    out_ref[...] = (
        g_ref[...].astype(jnp.float32)
        + rstd
        * (
            scaled
            - jnp.mean(scaled, axis=-1, keepdims=True)
            - xhat * jnp.mean(scaled * xhat, axis=-1, keepdims=True)
        )
    ).astype(jnp.bfloat16)


def finish(incoming, mine, other, x, gain, tile):
    rows, width = incoming.shape
    wide = pl.BlockSpec((tile, width), lambda i: (i, 0))
    return pl.pallas_call(
        finish_kernel,
        grid=(rows // tile,),
        in_specs=[wide, wide, wide, wide, pl.BlockSpec((1, width), lambda i: (0, 0))],
        out_specs=wide,
        out_shape=jax.ShapeDtypeStruct((rows, width), jnp.bfloat16),
        compiler_params=pltpu.CompilerParams(vmem_limit_bytes=8 * 1024 * 1024),
        cost_estimate=pl.CostEstimate(
            flops=20 * rows * width, bytes_accessed=10 * rows * width, transcendentals=0
        ),
    )(incoming, mine, other, x, gain)


def ask_tokens(seq_dev, slots, frames, sec, rep, peers):
    cap = slots.shape[1]
    per = -(-cap // peers)
    counts = TPF * jnp.sum(frames, axis=1)
    count = lax.dynamic_index_in_dim(counts, sec, 0, keepdims=False)
    wanted = lax.dynamic_index_in_dim(slots, sec, 0, keepdims=False)
    wanted = jnp.concatenate([wanted, jnp.zeros((per * peers - cap,), jnp.int32)])
    j = jnp.arange(per * peers)
    position = jnp.where(j < count, wanted - seq_dev * ((rep + j) % peers) + 1, 0)
    position = position.reshape(per, 1, peers)
    holder = jnp.arange(peers)
    turned = (jnp.arange(peers)[None, :] == ((holder - rep) % peers)[:, None]).astype(jnp.int32)
    requests = jnp.sum(position * turned[None], axis=2).T
    return lax.all_to_all(requests, "dp", 0, 0, tiled=True).reshape(-1)


def fetch_tokens(llm_grad, asked, cap, sec, ten, rep, peers):
    seq_dev, width = llm_grad.shape[1:]
    per = -(-cap // peers)
    pick = (asked[:, None] == jnp.arange(1, seq_dev + 1)[None, :]).astype(jnp.bfloat16)
    held = lax.dynamic_index_in_dim(llm_grad, sec, 0, keepdims=False)
    rows = dot(pick, held, 1, 0).astype(jnp.bfloat16)
    got = lax.all_to_all(rows, "dp", 0, 0, tiled=True)
    both = ("section", "tensor")
    first_own = lax.ppermute(got, both, [(0, 2), (1, 3)])
    first_other = lax.ppermute(got, both, [(0, 3), (1, 2)])
    second_other = lax.ppermute(got, both, [(2, 3), (3, 2)])
    half = width // 2
    row = jnp.arange(cap * 4)
    tok, part = row // 4, row % 4
    source = (
        ((part // 2 != ten).astype(jnp.int32) * 2 + part % 2) * (per * peers)
        + ((rep + tok) % peers) * per
        + tok // peers
    )
    spread = (source[:, None] == jnp.arange(4 * per * peers)[None, :]).astype(jnp.bfloat16)
    out = []
    for own, other in ((first_own, first_other), (got, second_other)):
        stacked = jnp.concatenate([own[:, :half], own[:, half:], other[:, :half], other[:, half:]])
        out.append(dot(spread, stacked, 1, 0).astype(jnp.bfloat16))
    return jnp.concatenate(out)


def reordered(left, stream):
    width = left.shape[1]
    sizes, axes = LAYOUTS[stream]
    split = left.reshape((2,) + sizes + (width >> BITS, -1))
    axes = (0,) + tuple(1 + a for a in axes) + (len(axes) + 1, len(axes) + 2)
    return split.transpose(axes).reshape(left.shape)


def after(value, *others):
    return lax.optimization_barrier((value, others))[0]


def reduce_weight_grads(left, right, first, second):
    width = left.shape[1]
    span = right.shape[2] // BITS
    lefts = [reordered(left, i) for i in range(BITS)]
    received = [[] for _ in range(BITS)]

    def group(i, lo, hi):
        total = lax.dot_general(
            lefts[i][:, lo:hi],
            right[:, :, i * span : (i + 1) * span],
            (((2,), (1,)), ((0,), (0,))),
            preferred_element_type=jnp.float32,
        )
        for piece in received[i]:
            total = total + piece[:, lo:hi].astype(jnp.float32)
        return total.astype(jnp.bfloat16)

    last, turns = None, {}
    for t in range(BITS):
        for place, streams in enumerate(SHARED[t]):
            if t == 0 and last is not None:
                lefts[place] = after(lefts[place], last)
            if t:
                for i in streams:
                    received[i][-1] = after(received[i][-1], last, turns.get((t, place)))
            sends = [group(i, width >> (t + 1), width >> t) for i in streams]
            last = sends[0] if len(sends) == 1 else jnp.concatenate(sends, axis=2)
            piece = lax.ppermute(last, "dp", neighbour_pairs(ORDERS[streams[0]][t]))
            for k, i in enumerate(streams):
                received[i].append(piece[:, :, k * span : (k + 1) * span])
        if t == 0:
            middle = first(last)
            turns[1, 0] = middle
        if t == 2:
            end = second(middle, last)
            turns[4, 0] = end[0]
    result = jnp.concatenate([group(i, 0, width >> BITS) for i in range(BITS)], axis=2)
    return result, middle, after(end, last)


def per_device(llm_grad, slots, frames, saved_in, ln_gain, w_in, w_out):
    peers = lax.axis_size("dp")
    sec = lax.axis_index("section")
    ten = lax.axis_index("tensor")
    rep = lax.axis_index("dp")
    micro_count, tok_rows, width = saved_in.shape[1:]
    rows = micro_count * tok_rows
    gain = ln_gain
    weight_in = w_in[0]
    weight_out = w_out[0]

    widen = saved_in[0].reshape(rows, width).astype(jnp.float32)
    centered = widen - jnp.mean(widen, axis=-1, keepdims=True)
    rstd = lax.rsqrt(jnp.mean(centered * centered, axis=-1, keepdims=True) + 1e-05)
    xhat = centered * rstd
    normed = (xhat * gain).astype(jnp.bfloat16)

    asked = ask_tokens(llm_grad.shape[1], slots, frames, sec, rep, peers)
    normed, asked = lax.optimization_barrier((normed, asked))
    upstream = lax.optimization_barrier(
        fetch_tokens(llm_grad, asked, slots.shape[1], sec, ten, rep, peers)
    )
    activ, slope = lax.optimization_barrier(gelu_and_slope(dot(normed, weight_in, 1, 0)))

    order = from_code(to_code(rep) ^ jnp.arange(peers))
    chunk = width // peers
    order = (order[:, None] * chunk + jnp.arange(chunk)[None, :]).reshape(-1)
    turn = (order[:, None] == jnp.arange(width)[None, :]).astype(jnp.bfloat16)

    x = saved_in[0].reshape(rows, width)

    def pre_gradient(incoming):
        return lax.optimization_barrier(
            (dot(incoming, weight_out, 1, 1) * slope).astype(jnp.bfloat16)
        )

    both = ("section", "tensor")
    first_own = lax.ppermute(got, both, [(0, 2), (1, 3)])
    first_other = lax.ppermute(got, both, [(0, 3), (1, 2)])
    second_other = lax.ppermute(got, both, [(2, 3), (3, 2)])
    half = width // 2
    row = jnp.arange(cap * 4)
    tok, part = row // 4, row % 4
    source = (
        ((part // 2 != ten).astype(jnp.int32) * 2 + part % 2) * (per * peers)
        + ((rep + tok) % peers) * per
        + tok // peers
    )
    spread = (source[:, None] == jnp.arange(4 * per * peers)[None, :]).astype(jnp.bfloat16)
    out = []
    for own, other in ((first_own, first_other), (got, second_other)):
        stacked = jnp.concatenate([own[:, :half], own[:, half:], other[:, :half], other[:, half:]])
        out.append(dot(spread, stacked, 1, 0).astype(jnp.bfloat16))
    return jnp.concatenate(out)


def reordered(left, stream):
    width = left.shape[1]
    sizes, axes = LAYOUTS[stream]
    split = left.reshape((2,) + sizes + (width >> BITS, -1))
    axes = (0,) + tuple(1 + a for a in axes) + (len(axes) + 1, len(axes) + 2)
    return split.transpose(axes).reshape(left.shape)


def after(value, *others):
    return lax.optimization_barrier((value, others))[0]


def reduce_weight_grads(left, right, first, second):
    width = left.shape[1]
    span = right.shape[2] // BITS
    lefts = [reordered(left, i) for i in range(BITS)]
    received = [[] for _ in range(BITS)]

    def group(i, lo, hi):
        total = lax.dot_general(
            lefts[i][:, lo:hi],
            right[:, :, i * span : (i + 1) * span],
            (((2,), (1,)), ((0,), (0,))),
            preferred_element_type=jnp.float32,
        )
        for piece in received[i]:
            total = total + piece[:, lo:hi].astype(jnp.float32)
        return total.astype(jnp.bfloat16)

    last, turns = None, {}
    for t in range(BITS):
        for place, streams in enumerate(SHARED[t]):
            if t == 0 and last is not None:
                lefts[place] = after(lefts[place], last)
            if t:
                for i in streams:
                    received[i][-1] = after(received[i][-1], last, turns.get((t, place)))
            sends = [group(i, width >> (t + 1), width >> t) for i in streams]
            last = sends[0] if len(sends) == 1 else jnp.concatenate(sends, axis=2)
            piece = lax.ppermute(last, "dp", neighbour_pairs(ORDERS[streams[0]][t]))
            for k, i in enumerate(streams):
                received[i].append(piece[:, :, k * span : (k + 1) * span])
        if t == 0:
            middle = first(last)
            turns[1, 0] = middle
        if t == 2:
            end = second(middle, last)
            turns[4, 0] = end[0]
    result = jnp.concatenate([group(i, 0, width >> BITS) for i in range(BITS)], axis=2)
    return result, middle, after(end, last)


def per_device(llm_grad, slots, frames, saved_in, ln_gain, w_in, w_out):
    peers = lax.axis_size("dp")
    sec = lax.axis_index("section")
    ten = lax.axis_index("tensor")
    rep = lax.axis_index("dp")
    micro_count, tok_rows, width = saved_in.shape[1:]
    rows = micro_count * tok_rows
    gain = ln_gain
    weight_in = w_in[0]
    weight_out = w_out[0]

    widen = saved_in[0].reshape(rows, width).astype(jnp.float32)
    centered = widen - jnp.mean(widen, axis=-1, keepdims=True)
    rstd = lax.rsqrt(jnp.mean(centered * centered, axis=-1, keepdims=True) + 1e-05)
    xhat = centered * rstd
    normed = (xhat * gain).astype(jnp.bfloat16)

    asked = ask_tokens(llm_grad.shape[1], slots, frames, sec, rep, peers)
    normed, asked = lax.optimization_barrier((normed, asked))
    upstream = lax.optimization_barrier(
        fetch_tokens(llm_grad, asked, slots.shape[1], sec, ten, rep, peers)
    )
    activ, slope = lax.optimization_barrier(gelu_and_slope(dot(normed, weight_in, 1, 0)))

    order = from_code(to_code(rep) ^ jnp.arange(peers))
    chunk = width // peers
    order = (order[:, None] * chunk + jnp.arange(chunk)[None, :]).reshape(-1)
    turn = (order[:, None] == jnp.arange(width)[None, :]).astype(jnp.bfloat16)

    x = saved_in[0].reshape(rows, width)

    def pre_gradient(incoming):
        return lax.optimization_barrier(
            (dot(incoming, weight_out, 1, 1) * slope).astype(jnp.bfloat16)
        )

    def operands(incoming, d_pre):
        left = jnp.stack([normed_t, dot(turn, incoming, 1, 1).astype(jnp.bfloat16)])
        return [reordered(left, i) for i in range(BITS)], jnp.stack([d_pre, activ])

    both = ("section", "tensor")
    d_pre = pre_gradient(upstream)
    partial = dot(d_pre, weight_in, 1, 1).astype(jnp.bfloat16)
    other = lax.ppermute(partial, both, [(2, 1), (3, 0)])
    terms, rest = [], ln_gain
    for _ in range(3):
        term = lax.reduce_precision(rest, exponent_bits=8, mantissa_bits=7)
        terms.append(jnp.broadcast_to(term, (16, width)).astype(jnp.bfloat16))
        rest = rest - term
    terms = after(jnp.concatenate(terms), normed)
    packed = jnp.concatenate([partial, upstream, x, terms])
    packed = lax.ppermute(packed, "section", [(1, 0)])
    mine, passed, later_x = (packed[k * rows : (k + 1) * rows] for k in range(3))
    later_gain = sum(
        packed[3 * rows + 16 * k : 3 * rows + 16 * k + 1].astype(jnp.float32) for k in range(3)
    )
    normed_t = dot(turn, after(normed, partial), 1, 1).astype(jnp.bfloat16)
    grad_last = finish(passed, mine, other, later_x, later_gain, tok_rows // 2)

    incoming = jnp.where(sec == 1, upstream, grad_last)
    d_pre = pre_gradient(incoming)
    incoming_t = dot(turn, incoming, 1, 1).astype(jnp.bfloat16)

    def partial_here(last):
        return dot(after(d_pre, last), weight_in, 1, 1).astype(jnp.bfloat16)

    def exchange(partial, last):
        return (
            lax.ppermute(after(partial, last), both, [(0, 1), (1, 0)]),
            lax.ppermute(after(grad_last, last), "section", [(0, 1)]),
        )

    reduced, partial, (other, returned) = reduce_weight_grads(
        jnp.stack([normed_t, incoming_t]), jnp.stack([d_pre, activ]), partial_here, exchange
    )
    grad_here = finish(incoming, partial, other, x, ln_gain, tok_rows // 2)
    results = jnp.where(sec == 1, returned, grad_here)
    return (
        results.reshape(1, micro_count, tok_rows, width),
        reduced[0][None],
        reduced[1].T[None],
    )


def solution(mesh):
    return jax.shard_map(
        per_device,
        mesh=mesh,
        in_specs=(
            P(None, "dp", "tensor"),
            P(None, "dp"),
            P(None, "dp"),
            P("section", None, "dp", None),
            P("section", None),
            P("section", None, "tensor"),
            P("section", "tensor", None),
        ),
        out_specs=(
            P("section", None, "dp", None),
            P("section", "dp", "tensor"),
            P("section", "tensor", "dp"),
        ),
        check_vma=False,
    )
```

```python
import functools

import jax
import jax.numpy as jnp
from jax import lax
from jax.experimental import pallas as pl
from jax.experimental.pallas import tpu as pltpu
from jax.sharding import PartitionSpec as P

TPF = 4
BITS = 5
ORDERS = ((0, 1, 2, 3, 4), (1, 2, 0, 3, 4), (2, 3, 4, 0, 1), (3, 4, 2, 0, 1), (4, 0, 1, 2, 3))
SHARED = (
    ((0,), (1,), (2,), (3,), (4,)),
    ((0,), (1,), (2,), (3,), (4,)),
    ((0, 3), (1,), (2,), (4,)),
    ((0, 1), (2, 3), (4,)),
    ((0, 1), (2, 3), (4,)),
)
LAYOUTS = (
    ((32,), (0,)),
    ((2, 4, 4), (1, 0, 2)),
    ((4, 8), (1, 0)),
    ((4, 2, 4), (2, 1, 0)),
    ((16, 2), (1, 0)),
)


def gelu_and_slope(a):
    square = a * a
    tangent = jnp.tanh(0.7978845608 * a * (1.0 + 0.044715 * square))
    half = 0.5 * (1.0 + tangent)
    slope = half + (0.5 * 0.7978845608) * a * (1.0 - tangent * tangent) * (
        1.0 + (3.0 * 0.044715) * square
    )
    return (a * half).astype(jnp.bfloat16), slope.astype(jnp.bfloat16)


def split_index(r):
    return r // 8, (r // 2) % 4, r % 2


def to_code(r):
    z, y, x = split_index(r)
    return ((z ^ (z >> 1)) << 3) | ((y ^ (y >> 1)) << 1) | x


def from_code(q):
    gz, gy, x = q >> 3, (q >> 1) & 3, q & 1
    return ((gz ^ (gz >> 1)) << 3) | ((gy ^ (gy >> 1)) << 1) | x


def neighbour_pairs(bit):
    return [(r, from_code(to_code(r) ^ (1 << (BITS - 1 - bit)))) for r in range(1 << BITS)]


def dot(a, b, ca, cb):
    return lax.dot_general(a, b, (((ca,), (cb,)), ((), ())), preferred_element_type=jnp.float32)


def finish_kernel(g_ref, mine_ref, other_ref, x_ref, gain_ref, out_ref):
    x = x_ref[...].astype(jnp.float32)
    centered = x - jnp.mean(x, axis=-1, keepdims=True)
    rstd = lax.rsqrt(jnp.mean(centered * centered, axis=-1, keepdims=True) + 1e-05)
    xhat = centered * rstd
    scaled = (mine_ref[...].astype(jnp.float32) + other_ref[...].astype(jnp.float32)) * gain_ref[...]
    out_ref[...] = (
        g_ref[...].astype(jnp.float32)
        + rstd
        * (
            scaled
            - jnp.mean(scaled, axis=-1, keepdims=True)
            - xhat * jnp.mean(scaled * xhat, axis=-1, keepdims=True)
        )
    ).astype(jnp.bfloat16)


def finish(incoming, mine, other, x, gain, tile):
    rows, width = incoming.shape
    wide = pl.BlockSpec((tile, width), lambda i: (i, 0))
    return pl.pallas_call(
        finish_kernel,
        grid=(rows // tile,),
        in_specs=[wide, wide, wide, wide, pl.BlockSpec((1, width), lambda i: (0, 0))],
        out_specs=wide,
        out_shape=jax.ShapeDtypeStruct((rows, width), jnp.bfloat16),
        compiler_params=pltpu.CompilerParams(vmem_limit_bytes=8 * 1024 * 1024),
        cost_estimate=pl.CostEstimate(
            flops=20 * rows * width, bytes_accessed=10 * rows * width, transcendentals=0
        ),
    )(incoming, mine, other, x, gain)


def ask_kernel(ids_ref, frames_ref, slots_ref, out_ref, *, seq_dev):
    sec, rep = ids_ref[0], ids_ref[1]
    peers, per = out_ref.shape
    cap = slots_ref.shape[1]
    count = frames_ref[sec, 0]
    for k in range(1, frames_ref.shape[1]):
        count = count + frames_ref[sec, k]
    wanted = jnp.where(sec == 0, slots_ref[0:1, :], slots_ref[1:2, :])
    j = lax.broadcasted_iota(jnp.int32, (1, cap), 1)
    holder = lax.rem(rep + j, peers)
    position = jnp.where(j < TPF * count, wanted - seq_dev * holder + 1, 0).astype(jnp.float32)
    here = lax.broadcasted_iota(jnp.int32, (peers, cap), 0) == holder
    column = lax.broadcasted_iota(jnp.int32, (peers, per), 1)
    out = jnp.zeros((peers, per), jnp.float32)
    for k in range(per):
        turn = here & (j >= k * peers) & (j < (k + 1) * peers)
        asked = jnp.sum(jnp.where(turn, position, 0.0), axis=1, keepdims=True)
        out = jnp.where(column == k, asked, out)
    out_ref[...] = out.astype(jnp.int32)


def ask_tokens(seq_dev, slots, frames, ids, peers):
    cap = slots.shape[1]
    per = -(-cap // peers)
    requests = pl.pallas_call(
        functools.partial(ask_kernel, seq_dev=seq_dev),
        grid_spec=pltpu.PrefetchScalarGridSpec(
            num_scalar_prefetch=2,
            grid=(1,),
            in_specs=[pl.BlockSpec(slots.shape, lambda i, *_: (0, 0))],
            out_specs=pl.BlockSpec((peers, per), lambda i, *_: (0, 0)),
        ),
        out_shape=jax.ShapeDtypeStruct((peers, per), jnp.int32),
    )(ids, frames, slots)
    return lax.all_to_all(requests, "dp", 0, 0, tiled=True)


def pick_kernel(ids_ref, asked_ref, held_ref, out_ref):
    peers, per = asked_ref.shape
    seq_dev = held_ref.shape[1]
    row = lax.broadcasted_iota(jnp.int32, (peers * per, 1), 0)
    spread = lax.broadcasted_iota(jnp.int32, (peers * per, peers), 1) == row // per
    asked = dot(
        spread.astype(jnp.float32).astype(jnp.bfloat16),
        asked_ref[...].astype(jnp.float32).astype(jnp.bfloat16),
        1,
        0,
    )
    place = jnp.zeros((peers * per, 1), jnp.float32)
    for k in range(per):
        place = jnp.where(row % per == k, asked[:, k : k + 1], place)
    positions = lax.broadcasted_iota(jnp.int32, (peers * per, seq_dev), 1) + 1
    pick = (place == positions.astype(jnp.float32)).astype(jnp.float32).astype(jnp.bfloat16)
    out_ref[...] = dot(pick, held_ref[0], 1, 0).astype(jnp.bfloat16)


def pick_rows(asked, llm_grad, ids):
    seq_dev, width = llm_grad.shape[1:]
    return pl.pallas_call(
        pick_kernel,
        grid_spec=pltpu.PrefetchScalarGridSpec(
            num_scalar_prefetch=1,
            grid=(1,),
            in_specs=[
                pl.BlockSpec(asked.shape, lambda i, *_: (0, 0)),
                pl.BlockSpec((1, seq_dev, width), lambda i, ids: (ids[0], 0, 0)),
            ],
            out_specs=pl.BlockSpec((asked.size, width), lambda i, *_: (0, 0)),
        ),
        out_shape=jax.ShapeDtypeStruct((asked.size, width), jnp.bfloat16),
    )(ids, asked, llm_grad)


def fetch_tokens(llm_grad, asked, cap, ids, ten, rep, peers):
    width = llm_grad.shape[2]
    per = -(-cap // peers)
    got = lax.all_to_all(pick_rows(asked, llm_grad, ids), "dp", 0, 0, tiled=True)
    both = ("section", "tensor")
    first_own = lax.ppermute(got, both, [(0, 2), (1, 3)])
    first_other = lax.ppermute(got, both, [(0, 3), (1, 2)])
    second_other = lax.ppermute(got, both, [(2, 3), (3, 2)])
    half = width // 2
    row = jnp.arange(cap * 4)
    tok, part = row // 4, row % 4
    source = (
        ((part // 2 != ten).astype(jnp.int32) * 2 + part % 2) * (per * peers)
        + ((rep + tok) % peers) * per
        + tok // peers
    )
    spread = (source[:, None] == jnp.arange(4 * per * peers)[None, :]).astype(jnp.bfloat16)
    out = []
    for own, other in ((first_own, first_other), (got, second_other)):
        stacked = jnp.concatenate([own[:, :half], own[:, half:], other[:, :half], other[:, half:]])
        out.append(dot(spread, stacked, 1, 0).astype(jnp.bfloat16))
    return jnp.concatenate(out), got


def reordered(left, stream):
    width = left.shape[1]
    sizes, axes = LAYOUTS[stream]
    split = left.reshape((2,) + sizes + (width >> BITS, -1))
    axes = (0,) + tuple(1 + a for a in axes) + (len(axes) + 1, len(axes) + 2)
    return split.transpose(axes).reshape(left.shape)


def after(value, *others):
    return lax.optimization_barrier((value, others))[0]


def reduce_weight_grads(left, right, first, second):
    width = left.shape[1]
    span = right.shape[2] // BITS
    lefts = [reordered(left, i) for i in range(BITS)]
    received = [[] for _ in range(BITS)]

    def group(i, lo, hi):
        total = lax.dot_general(
            lefts[i][:, lo:hi],
            right[:, :, i * span : (i + 1) * span],
            (((2,), (1,)), ((0,), (0,))),
            preferred_element_type=jnp.float32,
        )
        for piece in received[i]:
            total = total + piece[:, lo:hi].astype(jnp.float32)
        return total.astype(jnp.bfloat16)

    last, turns, started = None, {}, []
    for t in range(BITS):
        for place, streams in enumerate(SHARED[t]):
            if t:
                for i in streams:
                    received[i][-1] = after(received[i][-1], last, turns.get((t, place)))
            sends = [group(i, width >> (t + 1), width >> t) for i in streams]
            last = sends[0] if len(sends) == 1 else jnp.concatenate(sends, axis=2)
            started.append(last)
            piece = lax.ppermute(last, "dp", neighbour_pairs(ORDERS[streams[0]][t]))
            for k, i in enumerate(streams):
                received[i].append(piece[:, :, k * span : (k + 1) * span])
        if t == 0:
            middle = first(started)
            turns[1, 0] = middle
        if t == 2:
            end = second(middle, last)
            turns[4, 0] = end[0]
    result = jnp.concatenate([group(i, 0, width >> BITS) for i in range(BITS)], axis=2)
    return result, middle, after(end, last)


def per_device(llm_grad, slots, frames, saved_in, ln_gain, w_in, w_out):
    peers = lax.axis_size("dp")
    sec = lax.axis_index("section")
    ten = lax.axis_index("tensor")
    rep = lax.axis_index("dp")
    micro_count, tok_rows, width = saved_in.shape[1:]
    rows = micro_count * tok_rows
    gain = ln_gain
    weight_in = w_in[0]
    weight_out = w_out[0]

    widen = saved_in[0].reshape(rows, width).astype(jnp.float32)
    centered = widen - jnp.mean(widen, axis=-1, keepdims=True)
    rstd = lax.rsqrt(jnp.mean(centered * centered, axis=-1, keepdims=True) + 1e-05)
    xhat = centered * rstd
    normed = (xhat * gain).astype(jnp.bfloat16)

    ids = jnp.stack([sec, rep])
    asked = ask_tokens(llm_grad.shape[1], slots, frames, ids, peers)
    normed, asked = lax.optimization_barrier((normed, asked))
    upstream, got = fetch_tokens(llm_grad, asked, slots.shape[1], ids, ten, rep, peers)
    activ, slope = lax.optimization_barrier(gelu_and_slope(dot(normed, weight_in, 1, 0)))

    order = from_code(to_code(rep) ^ jnp.arange(peers))
    chunk = width // peers
    order = (order[:, None] * chunk + jnp.arange(chunk)[None, :]).reshape(-1)
    turn = (order[:, None] == jnp.arange(width)[None, :]).astype(jnp.bfloat16)

    normed_t = dot(turn, after(normed, got), 1, 1).astype(jnp.bfloat16)
    upstream = after(upstream, normed_t)
    x = saved_in[0].reshape(rows, width)

    def pre_gradient(incoming):
        return lax.optimization_barrier(
            (dot(incoming, weight_out, 1, 1) * slope).astype(jnp.bfloat16)
        )

    def operands(incoming, d_pre):
        left = jnp.stack([normed_t, dot(turn, incoming, 1, 1).astype(jnp.bfloat16)])
        return [reordered(left, i) for i in range(BITS)], jnp.stack([d_pre, activ])

    both = ("section", "tensor")
    d_pre = pre_gradient(upstream)
    partial = dot(d_pre, weight_in, 1, 1).astype(jnp.bfloat16)
    other = lax.ppermute(partial, both, [(2, 1), (3, 0)])
    terms, rest = [], ln_gain
    for _ in range(3):
        term = lax.reduce_precision(rest, exponent_bits=8, mantissa_bits=7)
        terms.append(jnp.broadcast_to(term, (16, width)).astype(jnp.bfloat16))
        rest = rest - term
    terms = after(jnp.concatenate(terms), normed)
    packed = jnp.concatenate([partial, upstream, x, terms])
    packed = lax.ppermute(packed, "section", [(1, 0)])
    mine, passed, later_x = (packed[k * rows : (k + 1) * rows] for k in range(3))
    later_gain = sum(
        packed[3 * rows + 16 * k : 3 * rows + 16 * k + 1].astype(jnp.float32) for k in range(3)
    )
    grad_last = finish(passed, mine, other, later_x, later_gain, tok_rows // 2)

    incoming = jnp.where(sec == 1, upstream, grad_last)
    d_pre = pre_gradient(incoming)
    incoming_t = dot(turn, incoming, 1, 1).astype(jnp.bfloat16)

    def partial_here(started):
        return dot(after(d_pre, *started), weight_in, 1, 1).astype(jnp.bfloat16)

    def exchange(partial, last):
        return (
            lax.ppermute(after(partial, last), both, [(0, 1), (1, 0)]),
            lax.ppermute(after(grad_last, last), "section", [(0, 1)]),
        )

    reduced, partial, (other, returned) = reduce_weight_grads(
        jnp.stack([normed_t, incoming_t]), jnp.stack([d_pre, activ]), partial_here, exchange
    )
    grad_here = finish(incoming, partial, other, x, ln_gain, tok_rows // 2)
    results = jnp.where(sec == 1, returned, grad_here)
    return (
        results.reshape(1, micro_count, tok_rows, width),
        reduced[0][None],
        reduced[1].T[None],
    )


def solution(mesh):
    return jax.shard_map(
        per_device,
        mesh=mesh,
        in_specs=(
            P(None, "dp", "tensor"),
            P(None, "dp"),
            P(None, "dp"),
            P("section", None, "dp", None),
            P("section", None),
            P("section", None, "tensor"),
            P("section", "tensor", None),
        ),
        out_specs=(
            P("section", None, "dp", None),
            P("section", "dp", "tensor"),
            P("section", "tensor", "dp"),
        ),
        check_vma=False,
    )
```

```python
import functools

import jax
import jax.numpy as jnp
from jax import lax
from jax.experimental import pallas as pl
from jax.experimental.pallas import tpu as pltpu
from jax.sharding import PartitionSpec as P

TPF = 4
BITS = 5
ORDERS = ((0, 1, 2, 3, 4), (1, 2, 0, 3, 4), (2, 3, 4, 0, 1), (3, 4, 2, 0, 1), (4, 0, 1, 2, 3))
SHARED = (
    ((0,), (1,), (2,), (3,), (4,)),
    ((0,), (1,), (2,), (3,), (4,)),
    ((0, 3), (1,), (2,), (4,)),
    ((0, 1), (2, 3), (4,)),
    ((0, 1), (2, 3), (4,)),
)
LAYOUTS = (
    ((32,), (0,)),
    ((2, 4, 4), (1, 0, 2)),
    ((4, 8), (1, 0)),
    ((4, 2, 4), (2, 1, 0)),
    ((16, 2), (1, 0)),
)


def gelu_and_slope(a):
    square = a * a
    tangent = jnp.tanh(0.7978845608 * a * (1.0 + 0.044715 * square))
    half = 0.5 * (1.0 + tangent)
    slope = half + (0.5 * 0.7978845608) * a * (1.0 - tangent * tangent) * (
        1.0 + (3.0 * 0.044715) * square
    )
    return (a * half).astype(jnp.bfloat16), slope.astype(jnp.bfloat16)


def split_index(r):
    return r // 8, (r // 2) % 4, r % 2


def to_code(r):
    z, y, x = split_index(r)
    return ((z ^ (z >> 1)) << 3) | ((y ^ (y >> 1)) << 1) | x


def from_code(q):
    gz, gy, x = q >> 3, (q >> 1) & 3, q & 1
    return ((gz ^ (gz >> 1)) << 3) | ((gy ^ (gy >> 1)) << 1) | x


def neighbour_pairs(bit):
    return [(r, from_code(to_code(r) ^ (1 << (BITS - 1 - bit)))) for r in range(1 << BITS)]


def dot(a, b, ca, cb):
    return lax.dot_general(a, b, (((ca,), (cb,)), ((), ())), preferred_element_type=jnp.float32)


def finish_kernel(g_ref, mine_ref, other_ref, x_ref, *refs):
    gain_refs, out_ref = refs[:-1], refs[-1]
    gain = gain_refs[0][0:1, :].astype(jnp.float32)
    for gain_ref in gain_refs[1:]:
        gain = gain + gain_ref[0:1, :].astype(jnp.float32)
    x = x_ref[...].astype(jnp.float32)
    centered = x - jnp.mean(x, axis=-1, keepdims=True)
    rstd = lax.rsqrt(jnp.mean(centered * centered, axis=-1, keepdims=True) + 1e-05)
    xhat = centered * rstd
    scaled = (mine_ref[...].astype(jnp.float32) + other_ref[...].astype(jnp.float32)) * gain
    out_ref[...] = (
        g_ref[...].astype(jnp.float32)
        + rstd
        * (
            scaled
            - jnp.mean(scaled, axis=-1, keepdims=True)
            - xhat * jnp.mean(scaled * xhat, axis=-1, keepdims=True)
        )
    ).astype(jnp.bfloat16)


def finish(operands, gains, rows, tile):
    width = operands[0][0].shape[1]
    wide = [
        pl.BlockSpec((tile, width), lambda i, k=start // tile: (k + i, 0)) for _, start in operands
    ]
    flat = [
        pl.BlockSpec((size, width), lambda i, k=start // size: (k, 0)) for _, start, size in gains
    ]
    return pl.pallas_call(
        finish_kernel,
        grid=(rows // tile,),
        in_specs=wide + flat,
        out_specs=pl.BlockSpec((tile, width), lambda i: (i, 0)),
        out_shape=jax.ShapeDtypeStruct((rows, width), jnp.bfloat16),
        compiler_params=pltpu.CompilerParams(vmem_limit_bytes=8 * 1024 * 1024),
        cost_estimate=pl.CostEstimate(
            flops=20 * rows * width, bytes_accessed=10 * rows * width, transcendentals=0
        ),
    )(*[array for array, _ in operands], *[array for array, _, _ in gains])


def ask_kernel(ids_ref, frames_ref, slots_ref, out_ref, *, seq_dev):
    sec, rep = ids_ref[0], ids_ref[1]
    peers, per = out_ref.shape
    cap = slots_ref.shape[1]
    count = frames_ref[sec, 0]
    for k in range(1, frames_ref.shape[1]):
        count = count + frames_ref[sec, k]
    wanted = jnp.where(sec == 0, slots_ref[0:1, :], slots_ref[1:2, :])
    j = lax.broadcasted_iota(jnp.int32, (1, cap), 1)
    holder = lax.rem(rep + j, peers)
    position = jnp.where(j < TPF * count, wanted - seq_dev * holder + 1, 0).astype(jnp.float32)
    here = lax.broadcasted_iota(jnp.int32, (peers, cap), 0) == holder
    column = lax.broadcasted_iota(jnp.int32, (peers, per), 1)
    out = jnp.zeros((peers, per), jnp.float32)
    for k in range(per):
        turn = here & (j >= k * peers) & (j < (k + 1) * peers)
        asked = jnp.sum(jnp.where(turn, position, 0.0), axis=1, keepdims=True)
        out = jnp.where(column == k, asked, out)
    out_ref[...] = out.astype(jnp.int32)


def ask_tokens(seq_dev, slots, frames, ids, peers):
    cap = slots.shape[1]
    per = -(-cap // peers)
    requests = pl.pallas_call(
        functools.partial(ask_kernel, seq_dev=seq_dev),
        grid_spec=pltpu.PrefetchScalarGridSpec(
            num_scalar_prefetch=2,
            grid=(1,),
            in_specs=[pl.BlockSpec(slots.shape, lambda i, *_: (0, 0))],
            out_specs=pl.BlockSpec((peers, per), lambda i, *_: (0, 0)),
        ),
        out_shape=jax.ShapeDtypeStruct((peers, per), jnp.int32),
    )(ids, frames, slots)
    return lax.all_to_all(requests, "dp", 0, 0, tiled=True)


def fetch_tokens(llm_grad, asked, cap, sec, ten, rep, peers):
    seq_dev, width = llm_grad.shape[1:]
    per = -(-cap // peers)
    pick = (asked.reshape(-1)[:, None] == jnp.arange(1, seq_dev + 1)[None, :]).astype(jnp.bfloat16)
    held = lax.dynamic_index_in_dim(llm_grad, sec, 0, keepdims=False)
    got = lax.all_to_all(dot(pick, held, 1, 0).astype(jnp.bfloat16), "dp", 0, 0, tiled=True)
    both = ("section", "tensor")
    first_own = lax.ppermute(got, both, [(0, 2), (1, 3)])
    first_other = lax.ppermute(got, both, [(0, 3), (1, 2)])
    second_other = lax.ppermute(got, both, [(2, 3), (3, 2)])
    half = width // 2
    row = jnp.arange(cap * 4)
    tok, part = row // 4, row % 4
    source = (
        ((part // 2 != ten).astype(jnp.int32) * 2 + part % 2) * (per * peers)
        + ((rep + tok) % peers) * per
        + tok // peers
    )
    spread = (source[:, None] == jnp.arange(4 * per * peers)[None, :]).astype(jnp.bfloat16)
    out = []
    for own, other in ((first_own, first_other), (got, second_other)):
        stacked = jnp.concatenate([own[:, :half], own[:, half:], other[:, :half], other[:, half:]])
        out.append(dot(spread, stacked, 1, 0).astype(jnp.bfloat16))
    return jnp.concatenate(out), got


def reordered(left, stream):
    width = left.shape[1]
    sizes, axes = LAYOUTS[stream]
    split = left.reshape((2,) + sizes + (width >> BITS, -1))
    axes = (0,) + tuple(1 + a for a in axes) + (len(axes) + 1, len(axes) + 2)
    return split.transpose(axes).reshape(left.shape)


def after(value, *others):
    return lax.optimization_barrier((value, others))[0]


def reduce_weight_grads(left, right, first, second):
    width = left.shape[1]
    span = right.shape[2] // BITS
    lefts = [reordered(left, i) for i in range(BITS)]
    received = [[] for _ in range(BITS)]

    def group(i, lo, hi):
        total = lax.dot_general(
            lefts[i][:, lo:hi],
            right[:, :, i * span : (i + 1) * span],
            (((2,), (1,)), ((0,), (0,))),
            preferred_element_type=jnp.float32,
        )
        for piece in received[i]:
            total = total + piece[:, lo:hi].astype(jnp.float32)
        return total.astype(jnp.bfloat16)

    last, turns, started = None, {}, []
    for t in range(BITS):
        for place, streams in enumerate(SHARED[t]):
            if t:
                for i in streams:
                    received[i][-1] = after(received[i][-1], last, turns.get((t, place)))
            sends = [group(i, width >> (t + 1), width >> t) for i in streams]
            last = sends[0] if len(sends) == 1 else jnp.concatenate(sends, axis=2)
            started.append(last)
            piece = lax.ppermute(last, "dp", neighbour_pairs(ORDERS[streams[0]][t]))
            for k, i in enumerate(streams):
                received[i].append(piece[:, :, k * span : (k + 1) * span])
        if t == 0:
            middle = first(started)
            turns[1, 0] = middle
        if t == 2:
            end = second(middle, last)
            turns[4, 0] = end[0]
    result = jnp.concatenate([group(i, 0, width >> BITS) for i in range(BITS)], axis=2)
    return result, middle, after(end, last)


def per_device(llm_grad, slots, frames, saved_in, ln_gain, w_in, w_out):
    peers = lax.axis_size("dp")
    sec = lax.axis_index("section")
    ten = lax.axis_index("tensor")
    rep = lax.axis_index("dp")
    micro_count, tok_rows, width = saved_in.shape[1:]
    rows = micro_count * tok_rows
    gain = ln_gain
    weight_in = w_in[0]
    weight_out = w_out[0]

    widen = saved_in[0].reshape(rows, width).astype(jnp.float32)
    centered = widen - jnp.mean(widen, axis=-1, keepdims=True)
    rstd = lax.rsqrt(jnp.mean(centered * centered, axis=-1, keepdims=True) + 1e-05)
    xhat = centered * rstd
    normed = (xhat * gain).astype(jnp.bfloat16)

    ids = jnp.stack([sec, rep])
    asked = ask_tokens(llm_grad.shape[1], slots, frames, ids, peers)
    normed, asked = lax.optimization_barrier((normed, asked))
    upstream, got = fetch_tokens(llm_grad, asked, slots.shape[1], sec, ten, rep, peers)
    activ, slope = lax.optimization_barrier(gelu_and_slope(dot(normed, weight_in, 1, 0)))

    order = from_code(to_code(rep) ^ jnp.arange(peers))
    chunk = width // peers
    order = (order[:, None] * chunk + jnp.arange(chunk)[None, :]).reshape(-1)
    turn = (order[:, None] == jnp.arange(width)[None, :]).astype(jnp.bfloat16)

    normed_t = dot(turn, after(normed, got), 1, 1).astype(jnp.bfloat16)
    upstream = after(upstream, normed_t)
    x = saved_in[0].reshape(rows, width)

    def pre_gradient(incoming):
        return lax.optimization_barrier(
            (dot(incoming, weight_out, 1, 1) * slope).astype(jnp.bfloat16)
        )

    def operands(incoming, d_pre):
        left = jnp.stack([normed_t, dot(turn, incoming, 1, 1).astype(jnp.bfloat16)])
        return [reordered(left, i) for i in range(BITS)], jnp.stack([d_pre, activ])

    both = ("section", "tensor")
    d_pre = pre_gradient(upstream)
    partial = dot(d_pre, weight_in, 1, 1).astype(jnp.bfloat16)
    other = lax.ppermute(partial, both, [(2, 1), (3, 0)])
    mine, passed, later_x, later_gain = (
        lax.ppermute(after(value, partial), "section", [(1, 0)])
        for value in (partial, upstream, x, ln_gain)
    )
    grad_last = finish(
        [(passed, 0), (mine, 0), (other, 0), (later_x, 0)], [(later_gain, 0, 1)], rows, tok_rows // 2
    )

    incoming = jnp.where(sec == 1, upstream, grad_last)
    d_pre = pre_gradient(incoming)
    incoming_t = dot(turn, incoming, 1, 1).astype(jnp.bfloat16)

    def partial_here(started):
        return dot(after(d_pre, *started), weight_in, 1, 1).astype(jnp.bfloat16)

    def exchange(partial, last):
        return (
            lax.ppermute(after(partial, last), both, [(0, 1), (1, 0)]),
            lax.ppermute(after(grad_last, last), "section", [(0, 1)]),
        )

    reduced, partial, (other, returned) = reduce_weight_grads(
        jnp.stack([normed_t, incoming_t]), jnp.stack([d_pre, activ]), partial_here, exchange
    )
    grad_here = finish(
        [(incoming, 0), (partial, 0), (other, 0), (x, 0)], [(ln_gain, 0, 1)], rows, tok_rows // 2
    )
    results = jnp.where(sec == 1, returned, grad_here)
    return (
        results.reshape(1, micro_count, tok_rows, width),
        reduced[0][None],
        reduced[1].T[None],
    )


def solution(mesh):
    return jax.shard_map(
        per_device,
        mesh=mesh,
        in_specs=(
            P(None, "dp", "tensor"),
            P(None, "dp"),
            P(None, "dp"),
            P("section", None, "dp", None),
            P("section", None),
            P("section", None, "tensor"),
            P("section", "tensor", None),
        ),
        out_specs=(
            P("section", None, "dp", None),
            P("section", "dp", "tensor"),
            P("section", "tensor", "dp"),
        ),
        check_vma=False,
    )
```

```python
import functools

import jax
import jax.numpy as jnp
from jax import lax
from jax.experimental import pallas as pl
from jax.experimental.pallas import tpu as pltpu
from jax.sharding import PartitionSpec as P

TPF = 4
BITS = 5
ORDERS = ((0, 1, 2, 3, 4), (1, 2, 0, 3, 4), (2, 3, 4, 0, 1), (3, 4, 2, 0, 1), (4, 0, 1, 2, 3))
SHARED = (
    ((0,), (1,), (2,), (3,), (4,)),
    ((0,), (1,), (2,), (3,), (4,)),
    ((0, 3), (1,), (2,), (4,)),
    ((0, 1), (2, 3), (4,)),
    ((0, 1), (2, 3), (4,)),
)
LAYOUTS = (
    ((32,), (0,)),
    ((2, 4, 4), (1, 0, 2)),
    ((4, 8), (1, 0)),
    ((4, 2, 4), (2, 1, 0)),
    ((16, 2), (1, 0)),
)


def gelu_and_slope(a):
    square = a * a
    tangent = jnp.tanh(0.7978845608 * a * (1.0 + 0.044715 * square))
    half = 0.5 * (1.0 + tangent)
    slope = half + (0.5 * 0.7978845608) * a * (1.0 - tangent * tangent) * (
        1.0 + (3.0 * 0.044715) * square
    )
    return (a * half).astype(jnp.bfloat16), slope.astype(jnp.bfloat16)


def split_index(r):
    return r // 8, (r // 2) % 4, r % 2


def to_code(r):
    z, y, x = split_index(r)
    return ((z ^ (z >> 1)) << 3) | ((y ^ (y >> 1)) << 1) | x


def from_code(q):
    gz, gy, x = q >> 3, (q >> 1) & 3, q & 1
    return ((gz ^ (gz >> 1)) << 3) | ((gy ^ (gy >> 1)) << 1) | x


def neighbour_pairs(bit):
    return [(r, from_code(to_code(r) ^ (1 << (BITS - 1 - bit)))) for r in range(1 << BITS)]


def dot(a, b, ca, cb):
    return lax.dot_general(a, b, (((ca,), (cb,)), ((), ())), preferred_element_type=jnp.float32)


def finish_kernel(g_ref, mine_ref, other_ref, x_ref, gain_ref, out_ref):
    x = x_ref[...].astype(jnp.float32)
    centered = x - jnp.mean(x, axis=-1, keepdims=True)
    rstd = lax.rsqrt(jnp.mean(centered * centered, axis=-1, keepdims=True) + 1e-05)
    xhat = centered * rstd
    scaled = (mine_ref[...].astype(jnp.float32) + other_ref[...].astype(jnp.float32)) * gain_ref[...]
    out_ref[...] = (
        g_ref[...].astype(jnp.float32)
        + rstd
        * (
            scaled
            - jnp.mean(scaled, axis=-1, keepdims=True)
            - xhat * jnp.mean(scaled * xhat, axis=-1, keepdims=True)
        )
    ).astype(jnp.bfloat16)


def finish(incoming, mine, other, x, gain, tile):
    rows, width = incoming.shape
    wide = pl.BlockSpec((tile, width), lambda i: (i, 0))
    return pl.pallas_call(
        finish_kernel,
        grid=(rows // tile,),
        in_specs=[wide, wide, wide, wide, pl.BlockSpec((1, width), lambda i: (0, 0))],
        out_specs=wide,
        out_shape=jax.ShapeDtypeStruct((rows, width), jnp.bfloat16),
        compiler_params=pltpu.CompilerParams(vmem_limit_bytes=8 * 1024 * 1024),
        cost_estimate=pl.CostEstimate(
            flops=20 * rows * width, bytes_accessed=10 * rows * width, transcendentals=0
        ),
    )(incoming, mine, other, x, gain)


def ask_kernel(ids_ref, frames_ref, slots_ref, out_ref, *, seq_dev):
    sec, rep = ids_ref[0], ids_ref[1]
    peers, per = out_ref.shape
    cap = slots_ref.shape[1]
    count = frames_ref[sec, 0]
    for k in range(1, frames_ref.shape[1]):
        count = count + frames_ref[sec, k]
    wanted = jnp.where(sec == 0, slots_ref[0:1, :], slots_ref[1:2, :])
    j = lax.broadcasted_iota(jnp.int32, (1, cap), 1)
    holder = lax.rem(rep + j, peers)
    position = jnp.where(j < TPF * count, wanted - seq_dev * holder + 1, 0).astype(jnp.float32)
    here = lax.broadcasted_iota(jnp.int32, (peers, cap), 0) == holder
    column = lax.broadcasted_iota(jnp.int32, (peers, per), 1)
    out = jnp.zeros((peers, per), jnp.float32)
    for k in range(per):
        turn = here & (j >= k * peers) & (j < (k + 1) * peers)
        asked = jnp.sum(jnp.where(turn, position, 0.0), axis=1, keepdims=True)
        out = jnp.where(column == k, asked, out)
    out_ref[...] = out.astype(jnp.int32)


def ask_tokens(seq_dev, slots, frames, ids, peers):
    cap = slots.shape[1]
    per = -(-cap // peers)
    requests = pl.pallas_call(
        functools.partial(ask_kernel, seq_dev=seq_dev),
        grid_spec=pltpu.PrefetchScalarGridSpec(
            num_scalar_prefetch=2,
            grid=(1,),
            in_specs=[pl.BlockSpec(slots.shape, lambda i, *_: (0, 0))],
            out_specs=pl.BlockSpec((peers, per), lambda i, *_: (0, 0)),
        ),
        out_shape=jax.ShapeDtypeStruct((peers, per), jnp.int32),
    )(ids, frames, slots)
    return lax.all_to_all(requests, "dp", 0, 0, tiled=True)


def fetch_tokens(llm_grad, asked, cap, sec, ten, rep, peers):
    seq_dev, width = llm_grad.shape[1:]
    per = -(-cap // peers)
    pick = (asked.reshape(-1)[:, None] == jnp.arange(1, seq_dev + 1)[None, :]).astype(jnp.bfloat16)
    held = lax.dynamic_index_in_dim(llm_grad, sec, 0, keepdims=False)
    got = lax.all_to_all(dot(pick, held, 1, 0).astype(jnp.bfloat16), "dp", 0, 0, tiled=True)
    both = ("section", "tensor")
    first_own = lax.ppermute(got, both, [(0, 2), (1, 3)])
    first_other = lax.ppermute(got, both, [(0, 3), (1, 2)])
    second_other = lax.ppermute(got, both, [(2, 3), (3, 2)])
    half = width // 2
    row = jnp.arange(cap * 4)
    tok, part = row // 4, row % 4
    source = (
        ((part // 2 != ten).astype(jnp.int32) * 2 + part % 2) * (per * peers)
        + ((rep + tok) % peers) * per
        + tok // peers
    )
    spread = (source[:, None] == jnp.arange(4 * per * peers)[None, :]).astype(jnp.bfloat16)
    out = []
    for own, other in ((first_own, first_other), (got, second_other)):
        stacked = jnp.concatenate([own[:, :half], own[:, half:], other[:, :half], other[:, half:]])
        out.append(dot(spread, stacked, 1, 0).astype(jnp.bfloat16))
    return jnp.concatenate(out), got


def reordered(left, stream):
    width = left.shape[1]
    sizes, axes = LAYOUTS[stream]
    split = left.reshape((2,) + sizes + (width >> BITS, -1))
    axes = (0,) + tuple(1 + a for a in axes) + (len(axes) + 1, len(axes) + 2)
    return split.transpose(axes).reshape(left.shape)


def after(value, *others):
    return lax.optimization_barrier((value, others))[0]


def reduce_weight_grads(left, right, first, second):
    width = left.shape[1]
    span = right.shape[2] // BITS
    lefts = [reordered(left, i) for i in range(BITS)]
    received = [[] for _ in range(BITS)]

    def group(i, lo, hi):
        total = lax.dot_general(
            lefts[i][:, lo:hi],
            right[:, :, i * span : (i + 1) * span],
            (((2,), (1,)), ((0,), (0,))),
            preferred_element_type=jnp.float32,
        )
        for piece in received[i]:
            total = total + piece[:, lo:hi].astype(jnp.float32)
        return total.astype(jnp.bfloat16)

    last, turns, started = None, {}, []
    for t in range(BITS):
        for place, streams in enumerate(SHARED[t]):
            if t:
                for i in streams:
                    received[i][-1] = after(received[i][-1], last, turns.get((t, place)))
            sends = [group(i, width >> (t + 1), width >> t) for i in streams]
            last = sends[0] if len(sends) == 1 else jnp.concatenate(sends, axis=2)
            started.append(last)
            piece = lax.ppermute(last, "dp", neighbour_pairs(ORDERS[streams[0]][t]))
            for k, i in enumerate(streams):
                received[i].append(piece[:, :, k * span : (k + 1) * span])
        if t == 0:
            middle = first(started)
            turns[1, 0] = middle
        if t == 2:
            end = second(middle, last)
            turns[4, 0] = end[0]
    result = jnp.concatenate([group(i, 0, width >> BITS) for i in range(BITS)], axis=2)
    return result, middle, after(end, last)


def per_device(llm_grad, slots, frames, saved_in, ln_gain, w_in, w_out):
    peers = lax.axis_size("dp")
    sec = lax.axis_index("section")
    ten = lax.axis_index("tensor")
    rep = lax.axis_index("dp")
    micro_count, tok_rows, width = saved_in.shape[1:]
    rows = micro_count * tok_rows
    gain = ln_gain
    weight_in = w_in[0]
    weight_out = w_out[0]

    widen = saved_in[0].reshape(rows, width).astype(jnp.float32)
    centered = widen - jnp.mean(widen, axis=-1, keepdims=True)
    rstd = lax.rsqrt(jnp.mean(centered * centered, axis=-1, keepdims=True) + 1e-05)
    xhat = centered * rstd
    normed = (xhat * gain).astype(jnp.bfloat16)

    ids = jnp.stack([sec, rep])
    asked = ask_tokens(llm_grad.shape[1], slots, frames, ids, peers)
    normed, asked = lax.optimization_barrier((normed, asked))
    upstream, got = fetch_tokens(llm_grad, asked, slots.shape[1], sec, ten, rep, peers)
    activ, slope = lax.optimization_barrier(gelu_and_slope(dot(normed, weight_in, 1, 0)))

    order = from_code(to_code(rep) ^ jnp.arange(peers))
    chunk = width // peers
    order = (order[:, None] * chunk + jnp.arange(chunk)[None, :]).reshape(-1)
    turn = (order[:, None] == jnp.arange(width)[None, :]).astype(jnp.bfloat16)

    normed_t = dot(turn, after(normed, got), 1, 1).astype(jnp.bfloat16)
    upstream = after(upstream, normed_t)
    x = saved_in[0].reshape(rows, width)

    def pre_gradient(incoming):
        return lax.optimization_barrier(
            (dot(incoming, weight_out, 1, 1) * slope).astype(jnp.bfloat16)
        )

    def operands(incoming, d_pre):
        left = jnp.stack([normed_t, dot(turn, incoming, 1, 1).astype(jnp.bfloat16)])
        return [reordered(left, i) for i in range(BITS)], jnp.stack([d_pre, activ])

    both = ("section", "tensor")
    d_pre = pre_gradient(upstream)
    partial = dot(d_pre, weight_in, 1, 1).astype(jnp.bfloat16)
    other = lax.ppermute(partial, both, [(2, 1), (3, 0)])
    terms, rest = [], ln_gain
    for _ in range(3):
        term = lax.reduce_precision(rest, exponent_bits=8, mantissa_bits=7)
        terms.append(jnp.broadcast_to(term, (16, width)).astype(jnp.bfloat16))
        rest = rest - term
    terms = after(jnp.concatenate(terms), normed)
    packed = jnp.concatenate([partial, upstream, x, terms])
    packed = lax.ppermute(packed, "section", [(1, 0)])
    mine, passed, later_x = (packed[k * rows : (k + 1) * rows] for k in range(3))
    later_gain = sum(
        packed[3 * rows + 16 * k : 3 * rows + 16 * k + 1].astype(jnp.float32) for k in range(3)
    )
    grad_last = finish(passed, mine, other, later_x, later_gain, tok_rows // 2)

    incoming = jnp.where(sec == 1, upstream, grad_last)
    d_pre = pre_gradient(incoming)
    incoming_t = dot(turn, incoming, 1, 1).astype(jnp.bfloat16)

    def partial_here(started):
        return dot(after(d_pre, *started), weight_in, 1, 1).astype(jnp.bfloat16)

    def exchange(partial, last):
        return (
            lax.ppermute(after(partial, last), both, [(0, 1), (1, 0)]),
            lax.ppermute(after(grad_last, last), "section", [(0, 1)]),
        )

    reduced, partial, (other, returned) = reduce_weight_grads(
        jnp.stack([normed_t, incoming_t]), jnp.stack([d_pre, activ]), partial_here, exchange
    )
    grad_here = finish(incoming, partial, other, x, ln_gain, tok_rows // 2)
    results = jnp.where(sec == 1, returned, grad_here)
    return (
        results.reshape(1, micro_count, tok_rows, width),
        reduced[0][None],
        reduced[1].T[None],
    )


def solution(mesh):
    return jax.shard_map(
        per_device,
        mesh=mesh,
        in_specs=(
            P(None, "dp", "tensor"),
            P(None, "dp"),
            P(None, "dp"),
            P("section", None, "dp", None),
            P("section", None),
            P("section", None, "tensor"),
            P("section", "tensor", None),
        ),
        out_specs=(
            P("section", None, "dp", None),
            P("section", "dp", "tensor"),
            P("section", "tensor", "dp"),
        ),
        check_vma=False,
    )
```

```python
import functools

import jax
import jax.numpy as jnp
from jax import lax
from jax.experimental import pallas as pl
from jax.experimental.pallas import tpu as pltpu
from jax.sharding import PartitionSpec as P

TPF = 4
BITS = 5
ORDERS = ((0, 1, 2, 3, 4), (1, 2, 0, 3, 4), (2, 3, 4, 0, 1), (3, 4, 2, 0, 1), (4, 0, 1, 2, 3))
SHARED = (
    ((0,), (1,), (2,), (3,), (4,)),
    ((0,), (1,), (2,), (3,), (4,)),
    ((0, 3), (1,), (2,), (4,)),
    ((0, 1), (2, 3), (4,)),
    ((0, 1), (2, 3), (4,)),
)
LAYOUTS = (
    ((32,), (0,)),
    ((2, 4, 4), (1, 0, 2)),
    ((4, 8), (1, 0)),
    ((4, 2, 4), (2, 1, 0)),
    ((16, 2), (1, 0)),
)


def gelu_and_slope(a):
    square = a * a
    tangent = jnp.tanh(0.7978845608 * a * (1.0 + 0.044715 * square))
    half = 0.5 * (1.0 + tangent)
    slope = half + (0.5 * 0.7978845608) * a * (1.0 - tangent * tangent) * (
        1.0 + (3.0 * 0.044715) * square
    )
    return (a * half).astype(jnp.bfloat16), slope.astype(jnp.bfloat16)


def split_index(r):
    return r // 8, (r // 2) % 4, r % 2


def to_code(r):
    z, y, x = split_index(r)
    return ((z ^ (z >> 1)) << 3) | ((y ^ (y >> 1)) << 1) | x


def from_code(q):
    gz, gy, x = q >> 3, (q >> 1) & 3, q & 1
    return ((gz ^ (gz >> 1)) << 3) | ((gy ^ (gy >> 1)) << 1) | x


def neighbour_pairs(bit):
    return [(r, from_code(to_code(r) ^ (1 << (BITS - 1 - bit)))) for r in range(1 << BITS)]


def dot(a, b, ca, cb):
    return lax.dot_general(a, b, (((ca,), (cb,)), ((), ())), preferred_element_type=jnp.float32)


def finish_kernel(g_ref, mine_ref, other_ref, x_ref, gain_ref, out_ref):
    x = x_ref[...].astype(jnp.float32)
    centered = x - jnp.mean(x, axis=-1, keepdims=True)
    rstd = lax.rsqrt(jnp.mean(centered * centered, axis=-1, keepdims=True) + 1e-05)
    xhat = centered * rstd
    scaled = (mine_ref[...].astype(jnp.float32) + other_ref[...].astype(jnp.float32)) * gain_ref[...]
    out_ref[...] = (
        g_ref[...].astype(jnp.float32)
        + rstd
        * (
            scaled
            - jnp.mean(scaled, axis=-1, keepdims=True)
            - xhat * jnp.mean(scaled * xhat, axis=-1, keepdims=True)
        )
    ).astype(jnp.bfloat16)


def finish(incoming, mine, other, x, gain, tile):
    rows, width = incoming.shape
    wide = pl.BlockSpec((tile, width), lambda i: (i, 0))
    return pl.pallas_call(
        finish_kernel,
        grid=(rows // tile,),
        in_specs=[wide, wide, wide, wide, pl.BlockSpec((1, width), lambda i: (0, 0))],
        out_specs=wide,
        out_shape=jax.ShapeDtypeStruct((rows, width), jnp.bfloat16),
        compiler_params=pltpu.CompilerParams(vmem_limit_bytes=8 * 1024 * 1024),
        cost_estimate=pl.CostEstimate(
            flops=20 * rows * width, bytes_accessed=10 * rows * width, transcendentals=0
        ),
    )(incoming, mine, other, x, gain)


def ask_kernel(ids_ref, frames_ref, slots_ref, out_ref, *, seq_dev):
    sec, rep = ids_ref[0], ids_ref[1]
    peers, per = out_ref.shape
    cap = slots_ref.shape[1]
    count = frames_ref[sec, 0]
    for k in range(1, frames_ref.shape[1]):
        count = count + frames_ref[sec, k]
    wanted = jnp.where(sec == 0, slots_ref[0:1, :], slots_ref[1:2, :])
    j = lax.broadcasted_iota(jnp.int32, (1, cap), 1)
    holder = lax.rem(rep + j, peers)
    position = jnp.where(j < TPF * count, wanted - seq_dev * holder + 1, 0).astype(jnp.float32)
    here = lax.broadcasted_iota(jnp.int32, (peers, cap), 0) == holder
    column = lax.broadcasted_iota(jnp.int32, (peers, per), 1)
    out = jnp.zeros((peers, per), jnp.float32)
    for k in range(per):
        turn = here & (j >= k * peers) & (j < (k + 1) * peers)
        asked = jnp.sum(jnp.where(turn, position, 0.0), axis=1, keepdims=True)
        out = jnp.where(column == k, asked, out)
    out_ref[...] = out.astype(jnp.int32)


def ask_tokens(seq_dev, slots, frames, ids, peers):
    cap = slots.shape[1]
    per = -(-cap // peers)
    requests = pl.pallas_call(
        functools.partial(ask_kernel, seq_dev=seq_dev),
        grid_spec=pltpu.PrefetchScalarGridSpec(
            num_scalar_prefetch=2,
            grid=(1,),
            in_specs=[pl.BlockSpec(slots.shape, lambda i, *_: (0, 0))],
            out_specs=pl.BlockSpec((peers, per), lambda i, *_: (0, 0)),
        ),
        out_shape=jax.ShapeDtypeStruct((peers, per), jnp.int32),
    )(ids, frames, slots)
    return lax.all_to_all(requests, "dp", 0, 0, tiled=True)


def pick_kernel(ids_ref, asked_ref, held_ref, out_ref):
    peers, per = asked_ref.shape
    seq_dev = held_ref.shape[1]
    row = lax.broadcasted_iota(jnp.int32, (peers * per, 1), 0)
    spread = lax.broadcasted_iota(jnp.int32, (peers * per, peers), 1) == row // per
    asked = dot(
        spread.astype(jnp.float32).astype(jnp.bfloat16),
        asked_ref[...].astype(jnp.float32).astype(jnp.bfloat16),
        1,
        0,
    )
    place = jnp.zeros((peers * per, 1), jnp.float32)
    for k in range(per):
        place = jnp.where(row % per == k, asked[:, k : k + 1], place)
    positions = lax.broadcasted_iota(jnp.int32, (peers * per, seq_dev), 1) + 1
    pick = (place == positions.astype(jnp.float32)).astype(jnp.float32).astype(jnp.bfloat16)
    out_ref[...] = dot(pick, held_ref[0], 1, 0).astype(jnp.bfloat16)


def pick_rows(asked, llm_grad, ids):
    seq_dev, width = llm_grad.shape[1:]
    return pl.pallas_call(
        pick_kernel,
        grid_spec=pltpu.PrefetchScalarGridSpec(
            num_scalar_prefetch=1,
            grid=(1,),
            in_specs=[
                pl.BlockSpec(asked.shape, lambda i, *_: (0, 0)),
                pl.BlockSpec((1, seq_dev, width), lambda i, ids: (ids[0], 0, 0)),
            ],
            out_specs=pl.BlockSpec((asked.size, width), lambda i, *_: (0, 0)),
        ),
        out_shape=jax.ShapeDtypeStruct((asked.size, width), jnp.bfloat16),
    )(ids, asked, llm_grad)


def fetch_tokens(llm_grad, asked, cap, ids, ten, rep, peers):
    width = llm_grad.shape[2]
    per = -(-cap // peers)
    got = lax.all_to_all(pick_rows(asked, llm_grad, ids), "dp", 0, 0, tiled=True)
    both = ("section", "tensor")
    first_own = lax.ppermute(got, both, [(0, 2), (1, 3)])
    first_other = lax.ppermute(got, both, [(0, 3), (1, 2)])
    second_other = lax.ppermute(got, both, [(2, 3), (3, 2)])
    half = width // 2
    row = jnp.arange(cap * 4)
    tok, part = row // 4, row % 4
    source = (
        ((part // 2 != ten).astype(jnp.int32) * 2 + part % 2) * (per * peers)
        + ((rep + tok) % peers) * per
        + tok // peers
    )
    spread = (source[:, None] == jnp.arange(4 * per * peers)[None, :]).astype(jnp.bfloat16)
    out = []
    for own, other in ((first_own, first_other), (got, second_other)):
        stacked = jnp.concatenate([own[:, :half], own[:, half:], other[:, :half], other[:, half:]])
        out.append(dot(spread, stacked, 1, 0).astype(jnp.bfloat16))
    return jnp.concatenate(out), got


def reordered(left, stream):
    width = left.shape[1]
    sizes, axes = LAYOUTS[stream]
    split = left.reshape((2,) + sizes + (width >> BITS, -1))
    axes = (0,) + tuple(1 + a for a in axes) + (len(axes) + 1, len(axes) + 2)
    return split.transpose(axes).reshape(left.shape)


def after(value, *others):
    return lax.optimization_barrier((value, others))[0]


def reduce_weight_grads(left, right, first, second):
    width = left.shape[1]
    span = right.shape[2] // BITS
    lefts = [reordered(left, i) for i in range(BITS)]
    received = [[] for _ in range(BITS)]

    def group(i, lo, hi):
        total = lax.dot_general(
            lefts[i][:, lo:hi],
            right[:, :, i * span : (i + 1) * span],
            (((2,), (1,)), ((0,), (0,))),
            preferred_element_type=jnp.float32,
        )
        for piece in received[i]:
            total = total + piece[:, lo:hi].astype(jnp.float32)
        return total.astype(jnp.bfloat16)

    last, turns, started = None, {}, []
    for t in range(BITS):
        for place, streams in enumerate(SHARED[t]):
            if t:
                for i in streams:
                    received[i][-1] = after(received[i][-1], last if t > 1 else None, turns.get((t, place)))
            sends = [group(i, width >> (t + 1), width >> t) for i in streams]
            last = sends[0] if len(sends) == 1 else jnp.concatenate(sends, axis=2)
            started.append(last)
            piece = lax.ppermute(last, "dp", neighbour_pairs(ORDERS[streams[0]][t]))
            for k, i in enumerate(streams):
                received[i].append(piece[:, :, k * span : (k + 1) * span])
        if t == 0:
            middle = first(started)
            turns[1, 0] = middle
        if t == 2:
            end = second(middle, last)
            turns[4, 0] = end[0]
    result = jnp.concatenate([group(i, 0, width >> BITS) for i in range(BITS)], axis=2)
    return result, middle, after(end, last)


def per_device(llm_grad, slots, frames, saved_in, ln_gain, w_in, w_out):
    peers = lax.axis_size("dp")
    sec = lax.axis_index("section")
    ten = lax.axis_index("tensor")
    rep = lax.axis_index("dp")
    micro_count, tok_rows, width = saved_in.shape[1:]
    rows = micro_count * tok_rows
    gain = ln_gain
    weight_in = w_in[0]
    weight_out = w_out[0]

    widen = saved_in[0].reshape(rows, width).astype(jnp.float32)
    centered = widen - jnp.mean(widen, axis=-1, keepdims=True)
    rstd = lax.rsqrt(jnp.mean(centered * centered, axis=-1, keepdims=True) + 1e-05)
    xhat = centered * rstd
    normed = (xhat * gain).astype(jnp.bfloat16)

    ids = jnp.stack([sec, rep])
    asked = ask_tokens(llm_grad.shape[1], slots, frames, ids, peers)
    normed, asked = lax.optimization_barrier((normed, asked))
    upstream, got = fetch_tokens(llm_grad, asked, slots.shape[1], ids, ten, rep, peers)
    activ, slope = lax.optimization_barrier(gelu_and_slope(dot(normed, weight_in, 1, 0)))

    order = from_code(to_code(rep) ^ jnp.arange(peers))
    chunk = width // peers
    order = (order[:, None] * chunk + jnp.arange(chunk)[None, :]).reshape(-1)
    turn = (order[:, None] == jnp.arange(width)[None, :]).astype(jnp.bfloat16)

    normed_t = dot(turn, after(normed, got), 1, 1).astype(jnp.bfloat16)
    upstream = after(upstream, normed_t)
    x = saved_in[0].reshape(rows, width)

    def pre_gradient(incoming):
        return lax.optimization_barrier(
            (dot(incoming, weight_out, 1, 1) * slope).astype(jnp.bfloat16)
        )

    def operands(incoming, d_pre):
        left = jnp.stack([normed_t, dot(turn, incoming, 1, 1).astype(jnp.bfloat16)])
        return [reordered(left, i) for i in range(BITS)], jnp.stack([d_pre, activ])

    both = ("section", "tensor")
    d_pre = pre_gradient(upstream)
    partial = dot(d_pre, weight_in, 1, 1).astype(jnp.bfloat16)
    other = lax.ppermute(partial, both, [(2, 1), (3, 0)])
    terms, rest = [], ln_gain
    for _ in range(3):
        term = lax.reduce_precision(rest, exponent_bits=8, mantissa_bits=7)
        terms.append(jnp.broadcast_to(term, (16, width)).astype(jnp.bfloat16))
        rest = rest - term
    terms = after(jnp.concatenate(terms), normed)
    packed = jnp.concatenate([partial, upstream, x, terms])
    packed = lax.ppermute(packed, "section", [(1, 0)])
    mine, passed, later_x = (packed[k * rows : (k + 1) * rows] for k in range(3))
    later_gain = sum(
        packed[3 * rows + 16 * k : 3 * rows + 16 * k + 1].astype(jnp.float32) for k in range(3)
    )
    grad_last = finish(passed, mine, other, later_x, later_gain, tok_rows // 2)

    incoming = jnp.where(sec == 1, upstream, grad_last)
    d_pre = pre_gradient(incoming)
    incoming_t = dot(turn, incoming, 1, 1).astype(jnp.bfloat16)

    def partial_here(started):
        return dot(after(d_pre, *started), weight_in, 1, 1).astype(jnp.bfloat16)

    def exchange(partial, last):
        return (
            lax.ppermute(after(partial, last), both, [(0, 1), (1, 0)]),
            lax.ppermute(after(grad_last, last), "section", [(0, 1)]),
        )

    reduced, partial, (other, returned) = reduce_weight_grads(
        jnp.stack([normed_t, incoming_t]), jnp.stack([d_pre, activ]), partial_here, exchange
    )
    grad_here = finish(incoming, partial, other, x, ln_gain, tok_rows // 2)
    results = jnp.where(sec == 1, returned, grad_here)
    return (
        results.reshape(1, micro_count, tok_rows, width),
        reduced[0][None],
        reduced[1].T[None],
    )


def solution(mesh):
    return jax.shard_map(
        per_device,
        mesh=mesh,
        in_specs=(
            P(None, "dp", "tensor"),
            P(None, "dp"),
            P(None, "dp"),
            P("section", None, "dp", None),
            P("section", None),
            P("section", None, "tensor"),
            P("section", "tensor", None),
        ),
        out_specs=(
            P("section", None, "dp", None),
            P("section", "dp", "tensor"),
            P("section", "tensor", "dp"),
        ),
        check_vma=False,
    )
```
